32 devices in a mesh: region: 4 (over z), batch: 8 (over y, x, core).
Axes of the slice: x: 2, y: 2, z: 4, core: 2. Of those that a mesh axis runs over, the one named last changes fastest.
Arguments:
- features: bfloat16 [32, 64, 1536], P('region', 'batch'), may hold values from -6 to 6
- mask: int32 [32, 512], P('region', 'batch'), may hold values 0 or 1
- owner: int32 [8], replicated, may hold values from 0 to 7, each once
- weight: bfloat16 [27, 36864], replicated, may hold values from -0.078125 to 0.078125
- bias: float32 [192], replicated, may hold values from -3 to 3
- cotangent: bfloat16 [32, 64, 1536], P('region', 'batch'), may hold values from -6 to 6
Outputs:
- activation: bfloat16 [32, 64, 1536], P('region', 'batch')
- grad_input: bfloat16 [32, 64, 1536], P('region', 'batch')
- grad_weight: bfloat16 [27, 36864], replicated
- grad_bias: float32 [192], replicated
The draws below stay inside these ranges and needn't reach their ends.
Inputs may be any that keep to these rules, and one draw needn't show every extreme that they name: owner is a permutation: each batch index holds exactly one tile of the grid of 4 rows by 2 tiles.
All inputs are finite; a program needn't handle non-finite values. No bound on the sum of `mask` on one device may be relied on, other than what follows from the above.
Results may differ from the reference program's by a relative error of at most 0.006.
Values may be sent and summed in bfloat16 or wider, within the bound.
No kernel may reach another device: no remote copies, remote signals or barrier semaphores. Data moves between devices by JAX's collectives and lax.ppermute only.
A program may use at most 128 MiB of HBM per device.

```python
import jax
import jax.numpy as jnp
from jax import lax

C = 192
ZD = 32
N_BATCH = 8


def plant(array, stream_key, least, high):
    longest = array.shape.index(max(array.shape))
    spots = []
    for shift in (0, 1):
        where = [jax.random.randint(jax.random.fold_in(stream_key, axis), (), 0, length) for axis, length in enumerate(array.shape)]
        where[longest] = (where[longest] + shift) % array.shape[longest]
        spots.append(tuple(where))
    return array.at[spots[0]].set(least).at[spots[1]].set(high)


def block_levels(own_key, extent, cuts, low, top_value):
    loudness, own = 1.0, jax.random.fold_in(own_key, 6)
    for position, shards_of in cuts:
        draws = jnp.exp(jax.random.uniform(jax.random.fold_in(own, position), (shards_of,), jnp.float32, low / len(cuts), top_value / len(cuts)))
        loudness = loudness * jnp.repeat(draws, extent[position] // shards_of).reshape([-1 if axis == position else 1 for axis in range(len(extent))])
    return loudness


def centred(stream_key, shape, scale, reach, shards=(), held_as=jnp.bfloat16):
    factor_of = block_levels(stream_key, shape, shards, -0.22, 0.18) if shards else 1.0
    result = jax.random.normal(stream_key, shape, jnp.float32) * scale * factor_of
    return jnp.minimum(jnp.maximum(result, -reach), reach).astype(held_as)


def setup_inputs(seed: int = 0) -> dict:
    streams_of = jax.random.split(jax.random.key(seed), 7)
    return {
        "features": centred(streams_of[0], (ZD, 8 * N_BATCH, 8 * C), 1.0, 6.0, ((0, 4), (1, 8))),
        "mask": plant((jax.random.randint(streams_of[1], (ZD, 64 * N_BATCH), 0, 5) < 3).astype(jnp.int32), jax.random.fold_in(streams_of[1], 1), 0, 1),
        "owner": jax.random.permutation(streams_of[2], N_BATCH).astype(jnp.int32),
        "weight": centred(streams_of[3], (27, C * C), (27 * C) ** -0.5, 0.078125),
        "bias": centred(streams_of[4], (C,), 0.5, 3.0, (), jnp.float32),
        "cotangent": centred(streams_of[5], (ZD, 8 * N_BATCH, 8 * C), 1.0, 6.0, ((0, 4), (1, 8))),
    }


LAYOUT = ("NDHWC", "DHWIO", "NDHWC")


def to_grid(values, owner, channels):
    depth = values.shape[0]
    tiles = owner.shape[0]
    columns = tiles // 4
    blocks = values.reshape(depth, tiles, 8, 8, channels)[:, owner]
    blocks = blocks.reshape(depth, 4, columns, 8, 8, channels)
    return blocks.transpose(0, 2, 3, 1, 4, 5).reshape(depth, columns * 8, 32, channels)


def from_grid(grid, owner):
    depth = grid.shape[0]
    channels = grid.shape[-1]
    tiles = owner.shape[0]
    columns = tiles // 4
    blocks = grid.reshape(depth, columns, 8, 4, 8, channels).transpose(0, 3, 1, 2, 4, 5)
    blocks = blocks.reshape(depth, tiles, 8, 8, channels)
    placed = jnp.zeros_like(blocks).at[:, owner].set(blocks)
    return placed.reshape(depth, tiles * 8, 8 * channels)


def convolve(field, kernel):
    return lax.conv_general_dilated(field[None], kernel, (1, 1, 1), "SAME", dimension_numbers=LAYOUT, precision=lax.Precision.HIGHEST)[0]


def reference(features, mask, owner, weight, bias, cotangent):
    channels = bias.shape[0]
    depth = features.shape[0]
    tiles = owner.shape[0]
    keep = to_grid(mask.reshape(depth, tiles * 8, 8), owner, 1).astype(jnp.float32)
    occupied = to_grid(features, owner, channels).astype(jnp.float32) * keep
    upstream = to_grid(cotangent, owner, channels).astype(jnp.float32)
    kernel = weight.astype(jnp.float32).reshape(3, 3, 3, channels, channels)
    pre = convolve(occupied, kernel) + bias
    sigma = jax.nn.sigmoid(pre)
    activation = (keep * pre * sigma).astype(jnp.bfloat16)
    grad_pre = (upstream * keep * sigma * (1.0 + pre * (1.0 - sigma))).astype(jnp.bfloat16)
    grad_wide = grad_pre.astype(jnp.float32)
    flipped = kernel[::-1, ::-1, ::-1].transpose(0, 1, 2, 4, 3)
    grad_input = (keep * convolve(grad_wide, flipped)).astype(jnp.bfloat16)
    padded = jnp.pad(occupied, ((1, 1), (1, 1), (1, 1), (0, 0)))
    width_x = occupied.shape[1]
    width_y = occupied.shape[2]
    flat = grad_wide.reshape(-1, channels)
    pieces = []
    for shift_z in range(3):
        for shift_x in range(3):
            for shift_y in range(3):
                window = padded[shift_z:shift_z + depth, shift_x:shift_x + width_x, shift_y:shift_y + width_y]
                pieces.append(jnp.dot(window.reshape(-1, channels).T, flat, precision=lax.Precision.HIGHEST))
    grad_weight = jnp.stack(pieces).reshape(27, channels * channels).astype(jnp.bfloat16)
    grad_bias = jnp.sum(flat, axis=0)
    return (from_grid(activation, owner), from_grid(grad_input, owner), grad_weight, grad_bias)
```

```python
import functools

import jax
import jax.numpy as jnp
from jax import lax
from jax.experimental import pallas as pl
from jax.experimental.pallas import tpu as pltpu
from jax.sharding import PartitionSpec as P

BF = jnp.bfloat16
F32 = jnp.float32
STEPS = ((0, 1), (0, -1), (1, 0), (-1, 0), (1, 1), (1, -1), (-1, 1), (-1, -1))
EDGE = 8
ROWS = 16
VMEM = pl.BlockSpec(memory_space=pltpu.VMEM)
SMEM = pl.BlockSpec(memory_space=pltpu.SMEM)
PARAMS = pltpu.CompilerParams(vmem_limit_bytes=48 * 2**20)


def pairs(count, flip):
    return [(i, i ^ flip) for i in range(count)]


def gather_windows(where, x_ref, recv_ref, rim, patch):
    depth, _, channels = x_ref.shape
    rim[:, 1:9, 8:16, :] = x_ref[...].reshape(depth, EDGE, EDGE, channels).astype(F32)
    lines = [recv_ref[where[n]].astype(F32) for n in range(8)]
    rim[:, 1:9, 16, :] = lines[0]
    rim[:, 1:9, 7, :] = lines[1]
    rim[:, 9, 8:16, :] = lines[2]
    rim[:, 0, 8:16, :] = lines[3]
    rim[:, 9, 16, :] = lines[4][:, 0]
    rim[:, 9, 7, :] = lines[5][:, 0]
    rim[:, 0, 16, :] = lines[6][:, 7]
    rim[:, 0, 7, :] = lines[7][:, 7]

    def plane(z, carry):
        for dx in range(3):
            for dy in range(3):
                seen = rim[z, dx : dx + 8, 7 + dy : 15 + dy, :]
                row = pl.multiple_of(z * 64, 64)
                patch[dx * 3 + dy, pl.ds(row, 64), :] = seen.reshape(64, channels).astype(BF)
        return carry

    lax.fori_loop(0, depth, plane, 0)


def forward_kernel(leaf_units, n_leaves, where, x_ref, recv_ref, w_ref, bias_ref, cot_ref,
                   act_ref, gp_ref, gb_ref, gw_ref, rim, patch):
    voxels, channels = cot_ref.shape
    gather_windows(where, x_ref, recv_ref, rim, patch)
    pre = jnp.broadcast_to(bias_ref[...], (voxels, channels))
    for dz in range(3):
        for k in range(9):
            pre += jnp.dot(
                patch[k, dz * 64 : dz * 64 + voxels, :],
                w_ref[dz * 9 + k],
                preferred_element_type=F32,
            )
    sigma = jax.nn.sigmoid(pre)
    act_ref[...] = (pre * sigma).astype(BF)
    grad = (cot_ref[...].astype(F32) * sigma * (1.0 + pre * (1.0 - sigma))).astype(BF)
    gp_ref[...] = grad
    gb_ref[...] = jnp.sum(grad.astype(F32), axis=0, keepdims=True)
    half = channels // 2
    per_offset = half // ROWS
    lanes = 2 * channels // 128
    code = (where[8], where[9])

    def put(unit, value):
        leaf, inner = divmod(unit, leaf_units)
        colour = (leaf // (n_leaves // 4)) % 2
        gw_ref[(leaf ^ code[colour]) * leaf_units + inner] = value

    for dz in range(3):
        for k in range(9):
            o = dz * 9 + k
            part = lax.dot_general(
                patch[k, dz * 64 : dz * 64 + voxels, :],
                grad,
                (((0,), (0,)), ((), ())),
                preferred_element_type=F32,
            )
            wide = jnp.concatenate([part[:half], part[half:]], axis=1).astype(BF)
            for rows in range(per_offset):
                for lane in range(lanes):
                    put(
                        (o * per_offset + rows) * lanes + lane,
                        wide[rows * ROWS : (rows + 1) * ROWS, lane * 128 : (lane + 1) * 128],
                    )
    for unit in range(27 * per_offset * lanes, leaf_units * n_leaves):
        put(unit, jnp.zeros((ROWS, 128), BF))


def input_kernel(where, x_ref, recv_ref, w_ref, out_ref, rim, patch):
    voxels, channels = out_ref.shape
    gather_windows(where, x_ref, recv_ref, rim, patch)
    total = jnp.zeros((voxels, channels), F32)
    for dz in range(3):
        for k in range(9):
            total += lax.dot_general(
                patch[8 - k, (2 - dz) * 64 : (2 - dz) * 64 + voxels, :],
                w_ref[dz * 9 + k],
                (((1,), (1,)), ((), ())),
                preferred_element_type=F32,
            )
    out_ref[...] = total.astype(BF)


def unfold_kernel(leaf_units, n_leaves, where, near_ref, far_ref, out_ref, flat):
    code = (where[8], where[9])
    half_leaves = n_leaves // 2

    def spread(ref, first_leaf):
        for leaf in range(half_leaves):
            rel = first_leaf + leaf
            colour = (rel // (n_leaves // 4)) % 2
            base = (rel ^ code[colour]) * leaf_units

            def one(u, carry, base=base, leaf=leaf):
                row = pl.multiple_of((base + u) * ROWS, ROWS)
                flat[pl.ds(row, ROWS), :] = ref[leaf * leaf_units + u].astype(F32)
                return carry

            lax.fori_loop(0, leaf_units, one, 0, unroll=True)

    spread(near_ref, 0)
    spread(far_ref, half_leaves)
    pitch = flat.shape[0] // 32
    low = lax.broadcasted_iota(jnp.int32, (8, 128), 1) < 64

    def turned(x):
        return pltpu.roll(x, 64, 1)

    def block(base, group):
        rows = []
        for i in range(2):
            rows.append(
                [
                    flat[pl.ds(base + i + lane * ROWS + group * 8 * pitch, 8, stride=pitch), :]
                    for lane in range(3)
                ]
            )
        (a0, a1, a2), (b0, b1, b2) = rows
        rb0, rb1, ra1, ra2 = turned(b0), turned(b1), turned(a1), turned(a2)
        return (
            a0,
            jnp.where(low, a1, rb0),
            jnp.where(low, rb0, rb1),
            jnp.where(low, ra1, ra2),
            jnp.where(low, ra2, b1),
            b2,
        )

    count = out_ref.shape[0]
    span = out_ref.shape[1] // 2

    def pair(m, carry):
        i = m * 2
        base = (i // ROWS) * (3 * ROWS) + i % ROWS
        for top in range(0, count, 16):
            tiles = [block(base, top // 8), block(base, top // 8 + 1)]
            high = min(16, count - top)
            for n in range(6):
                both = jnp.concatenate([tiles[0][n], tiles[1][n]], axis=0).astype(BF)
                lane = pl.multiple_of((n // 3) * span + m * 384 + (n % 3) * 128, 128)
                out_ref[top : top + high, pl.ds(lane, 128)] = both[:high]
        return carry

    lax.fori_loop(0, span // 384, pair, 0, unroll=2)


def body(features, mask, owner, weight, bias, cotangent):
    channels = bias.shape[0]
    depth = features.shape[0]
    voxels = depth * 64
    regions = lax.axis_size("region")
    tiles = lax.axis_size("batch")
    bits = tiles.bit_length() - 1
    mine = lax.axis_index("batch")
    slab = lax.axis_index("region")

    columns = tiles // 4
    slots = jnp.arange(tiles, dtype=jnp.int32)
    places = jnp.sum(jnp.where(owner[:, None] == slots[None, :], slots[:, None], 0), axis=0)
    my_place = jnp.sum(jnp.where(slots == mine, places, 0))
    step_x = places % columns - my_place % columns
    step_y = places // columns - my_place // columns
    near = (jnp.abs(step_x) <= 1) & (jnp.abs(step_y) <= 1) & (slots != mine)
    wanted = jnp.where(
        step_y == 1, 0, jnp.where(step_y == -1, 1, jnp.where(step_x == 1, 2, 3))
    )
    send = (near[:, None] & (wanted[:, None] == jnp.arange(4)[None, :])).astype(BF)
    sources = [
        jnp.sum(jnp.where((step_x == x) & (step_y == y), slots - mine, 0)) + mine
        for x, y in STEPS
    ]

    orders = (tuple(range(1, bits)), tuple(range(bits - 1, 0, -1)))
    codes = []
    for order in orders:
        code = (mine & 1) << bits
        for n, bit in enumerate(order):
            code = code | (((mine >> bit) & 1) << (bits - 2 - n))
        codes.append(code)
    where = jnp.stack(sources + codes).astype(jnp.int32)
    n_leaves = 2 * tiles
    units = 27 * (channels // 2 // ROWS) * (2 * channels // 128)
    leaf_units = -(-units // n_leaves)

    def rims(planes):
        up = lax.ppermute(planes[-1:], "region", [(i, i + 1) for i in range(regions - 1)])
        down = lax.ppermute(planes[:1], "region", [(i + 1, i) for i in range(regions - 1)])
        return jnp.concatenate([up, planes, down], axis=0)

    def neighbours(planes):
        grid = planes.reshape(planes.shape[0], EDGE, EDGE, channels)
        lines = jnp.stack([grid[:, :, 7], grid[:, :, 0], grid[:, 7], grid[:, 0]])
        chosen = jnp.einsum("qk,kzxc->qzxc", send, lines, preferred_element_type=F32)
        return lax.all_to_all(chosen.astype(BF), "batch", 0, 0, tiled=True)

    scratch = [
        pltpu.VMEM((depth + 2, 10, 24, channels), F32),
        pltpu.VMEM((9, (depth + 2) * 64, channels), BF),
    ]
    keep = mask.reshape(depth, 64, 1).astype(BF)
    occupied = rims(features.reshape(depth, 64, channels) * keep)
    upstream = (cotangent.reshape(depth, 64, channels) * keep).reshape(voxels, channels)
    kernel = weight.reshape(27, channels, channels)

    act, grad, bias_terms, terms = pl.pallas_call(
        functools.partial(forward_kernel, leaf_units, n_leaves),
        out_shape=(
            jax.ShapeDtypeStruct((voxels, channels), BF),
            jax.ShapeDtypeStruct((voxels, channels), BF),
            jax.ShapeDtypeStruct((1, channels), F32),
            jax.ShapeDtypeStruct((n_leaves * leaf_units, ROWS, 128), BF),
        ),
        in_specs=[SMEM, VMEM, VMEM, VMEM, VMEM, VMEM],
        out_specs=(VMEM, VMEM, VMEM, VMEM),
        scratch_shapes=scratch,
        compiler_params=PARAMS,
        cost_estimate=pl.CostEstimate(
            flops=4 * 27 * voxels * channels * channels, bytes_accessed=6 << 20, transcendentals=voxels * channels
        ),
    )(where, occupied, neighbours(occupied), kernel, bias.reshape(1, channels), upstream)

    def halve(x, axis, count, flip):
        half = x.shape[0] // 2
        got = lax.ppermute(x[half:].astype(BF), axis, pairs(count, flip))
        return x[:half].astype(F32) + got.astype(F32)

    parts = halve(terms, "batch", tiles, 1)
    split = parts.shape[0] // 2
    colours = [parts[:split], parts[split:]]
    for step in range(bits - 1):
        colours = [halve(c, "batch", tiles, 1 << o[step]) for c, o in zip(colours, orders)]
    last = jnp.concatenate(colours, axis=0)
    share = -(-last.shape[0] // regions)
    spare = share * regions - last.shape[0]
    last = jnp.pad(last, ((0, spare), (0, 0), (0, 0))).reshape(regions, share, ROWS, 128)
    flips = sorted(range(1, regions), key=lambda f: -f)
    total = lax.dynamic_index_in_dim(last, slab, 0, False)
    for flip in flips:
        piece = lax.dynamic_index_in_dim(last, slab ^ flip, 0, False).astype(BF)
        total = total + lax.ppermute(piece, "region", pairs(regions, flip)).astype(F32)
    total = total.astype(BF)

    held = [total] + [
        lax.ppermute(total, "region", pairs(regions, flip)) for flip in range(1, regions)
    ]
    whole = jnp.zeros((regions, share, ROWS, 128), BF)
    for flip, block in enumerate(held):
        whole = lax.dynamic_update_index_in_dim(whole, block, slab ^ flip, 0)
    whole = whole.reshape(regions * share, ROWS, 128)
    colours = [whole[:leaf_units], whole[leaf_units : 2 * leaf_units]]
    for step in reversed(range(bits - 1)):
        colours = [
            jnp.concatenate([c, lax.ppermute(c, "batch", pairs(tiles, 1 << o[step]))], axis=0)
            for c, o in zip(colours, orders)
        ]
    own = jnp.concatenate(colours, axis=0)
    other = lax.ppermute(own, "batch", pairs(tiles, 1))
    kernel_grad = pl.pallas_call(
        functools.partial(unfold_kernel, leaf_units, n_leaves),
        out_shape=jax.ShapeDtypeStruct((27, channels * channels), BF),
        in_specs=[SMEM, VMEM, VMEM],
        out_specs=VMEM,
        scratch_shapes=[pltpu.VMEM((32 * units // 27 * ROWS, 128), F32)],
        compiler_params=PARAMS,
    )(where, own, other)

    total_bias = bias_terms
    for bit in range(bits):
        total_bias = total_bias + lax.ppermute(total_bias, "batch", pairs(tiles, 1 << bit))
    for bit in range(regions.bit_length() - 1):
        total_bias = total_bias + lax.ppermute(total_bias, "region", pairs(regions, 1 << bit))

    full_grad = rims(grad.reshape(depth, 64, channels))
    grad_input = pl.pallas_call(
        input_kernel,
        out_shape=jax.ShapeDtypeStruct((voxels, channels), BF),
        in_specs=[SMEM, VMEM, VMEM, VMEM],
        out_specs=VMEM,
        scratch_shapes=scratch,
        compiler_params=PARAMS,
        cost_estimate=pl.CostEstimate(
            flops=2 * 27 * voxels * channels * channels, bytes_accessed=3 << 20, transcendentals=0
        ),
    )(where, full_grad, neighbours(full_grad), kernel)

    def placed(rows):
        return (rows.reshape(depth, 64, channels) * keep).reshape(features.shape)

    return placed(act), placed(grad_input), kernel_grad, total_bias.reshape(channels)


def solution(mesh):
    split = P("region", "batch", None)
    return jax.shard_map(
        body,
        mesh=mesh,
        in_specs=(split, P("region", "batch"), P(), P(), P(), split),
        out_specs=(split, split, P(), P()),
        check_vma=False,
    )
```

```python
import functools

import jax
import jax.numpy as jnp
from jax import lax
from jax.experimental import pallas as pl
from jax.experimental.pallas import tpu as pltpu
from jax.sharding import PartitionSpec as P

BF = jnp.bfloat16
F32 = jnp.float32
STEPS = ((0, 1), (0, -1), (1, 0), (-1, 0), (1, 1), (1, -1), (-1, 1), (-1, -1))
EDGE = 8
ROWS = 16
VMEM = pl.BlockSpec(memory_space=pltpu.VMEM)
SMEM = pl.BlockSpec(memory_space=pltpu.SMEM)
PARAMS = pltpu.CompilerParams(vmem_limit_bytes=48 * 2**20)


def pairs(count, flip):
    return [(i, i ^ flip) for i in range(count)]


def placed_at(owner):
    tiles = owner.shape[0]
    mine = lax.axis_index("batch")
    place = 0
    for q in range(tiles):
        place = place + jnp.where(owner[q] == mine, q, 0)
    return place, tiles // 4, 4


def neighbour(spot, step):
    place, columns, rows = spot
    column = place % columns + step[0]
    row = place // columns + step[1]
    there = (column >= 0) & (column < columns) & (row >= 0) & (row < rows)
    return there, jnp.where(there, place + step[1] * columns + step[0], place)


def leaf_codes(tiles):
    bits = tiles.bit_length() - 1
    mine = lax.axis_index("batch")
    codes = []
    for order in send_orders(tiles):
        code = (mine & 1) << bits
        for n, bit in enumerate(order):
            code = code | (((mine >> bit) & 1) << (bits - 2 - n))
        codes.append(code)
    return codes


def send_orders(tiles):
    bits = tiles.bit_length() - 1
    return tuple(range(1, bits)), tuple(range(bits - 1, 0, -1))


def lines_kernel(owner, below_ref, x_ref, above_ref, extra_ref, out_ref, rim):
    depth, _, channels = x_ref.shape
    grid = (EDGE, EDGE, channels)
    rim[0] = below_ref[0].reshape(grid).astype(F32)
    rim[1 : depth + 1] = x_ref[...].reshape((depth,) + grid).astype(F32)
    rim[depth + 1] = above_ref[0].reshape(grid).astype(F32)
    out_ref[...] = jnp.zeros(out_ref.shape, BF)
    for q in range(out_ref.shape[0]):
        out_ref[q, depth + 2] = extra_ref[...]
    spot = placed_at(owner)
    lines = {
        (0, 1): rim[:, :, 7, :].astype(BF),
        (0, -1): rim[:, :, 0, :].astype(BF),
        (1, 0): rim[:, 7].astype(BF),
        (-1, 0): rim[:, 0].astype(BF),
    }
    for step in STEPS:
        there, place = neighbour(spot, step)
        line = lines[(0, step[1]) if step[1] else step]

        @pl.when(there)
        def _(line=line, place=place):
            out_ref[owner[place], : depth + 2] = line


def gather_windows(owner, below_ref, x_ref, above_ref, recv_ref, rim, patch):
    depth, _, channels = x_ref.shape
    grid = (EDGE, EDGE, channels)
    rim[0, 1:9, 8:16, :] = below_ref[0].reshape(grid).astype(F32)
    rim[1 : depth + 1, 1:9, 8:16, :] = x_ref[...].reshape((depth,) + grid).astype(F32)
    rim[depth + 1, 1:9, 8:16, :] = above_ref[0].reshape(grid).astype(F32)
    spot = placed_at(owner)
    lines = [
        recv_ref[owner[neighbour(spot, step)[1]], : depth + 2].astype(F32) for step in STEPS
    ]
    rim[:, 1:9, 16, :] = lines[0]
    rim[:, 1:9, 7, :] = lines[1]
    rim[:, 9, 8:16, :] = lines[2]
    rim[:, 0, 8:16, :] = lines[3]
    rim[:, 9, 16, :] = lines[4][:, 0]
    rim[:, 9, 7, :] = lines[5][:, 0]
    rim[:, 0, 16, :] = lines[6][:, 7]
    rim[:, 0, 7, :] = lines[7][:, 7]

    def plane(z, carry):
        for dx in range(3):
            for dy in range(3):
                seen = rim[z, dx : dx + 8, 7 + dy : 15 + dy, :]
                row = pl.multiple_of(z * 64, 64)
                patch[dx * 3 + dy, pl.ds(row, 64), :] = seen.reshape(64, channels).astype(BF)
        return carry

    lax.fori_loop(0, depth + 2, plane, 0)


def forward_kernel(leaf_units, n_leaves, owner, below_ref, x_ref, above_ref, recv_ref, w_ref,
                   bias_ref, cot_ref, act_ref, gp_ref, gb_ref, gw_ref, rim, patch):
    voxels, channels = cot_ref.shape
    gather_windows(owner, below_ref, x_ref, above_ref, recv_ref, rim, patch)
    pre = jnp.broadcast_to(bias_ref[...], (voxels, channels))
    for dz in range(3):
        for k in range(9):
            pre += jnp.dot(
                patch[k, dz * 64 : dz * 64 + voxels, :],
                w_ref[dz * 9 + k],
                preferred_element_type=F32,
            )
    sigma = jax.nn.sigmoid(pre)
    act_ref[...] = (pre * sigma).astype(BF)
    grad = (cot_ref[...].astype(F32) * sigma * (1.0 + pre * (1.0 - sigma))).astype(BF)
    gp_ref[...] = grad
    rest = jnp.sum(grad.astype(F32), axis=0, keepdims=True)
    slices = []
    for _ in range(3):
        slices.append(rest.astype(BF).astype(F32))
        rest = rest - slices[-1]
    slices.append(jnp.zeros((5, channels), F32))
    gb_ref[...] = jnp.concatenate(slices, axis=0).astype(BF)
    half = channels // 2
    per_offset = half // ROWS
    lanes = 2 * channels // 128
    code = leaf_codes(owner.shape[0])

    def put(unit, value):
        leaf, inner = divmod(unit, leaf_units)
        colour = (leaf // (n_leaves // 4)) % 2
        gw_ref[(leaf ^ code[colour]) * leaf_units + inner] = value

    for dz in range(3):
        for k in range(9):
            o = dz * 9 + k
            part = lax.dot_general(
                patch[k, dz * 64 : dz * 64 + voxels, :],
                grad,
                (((0,), (0,)), ((), ())),
                preferred_element_type=F32,
            )
            wide = jnp.concatenate([part[:half], part[half:]], axis=1).astype(BF)
            for rows in range(per_offset):
                for lane in range(lanes):
                    put(
                        (o * per_offset + rows) * lanes + lane,
                        wide[rows * ROWS : (rows + 1) * ROWS, lane * 128 : (lane + 1) * 128],
                    )
    for unit in range(27 * per_offset * lanes, leaf_units * n_leaves):
        put(unit, jnp.zeros((ROWS, 128), BF))


def input_kernel(owner, below_ref, x_ref, above_ref, recv_ref, w_ref, out_ref, gb_ref, rim, patch):
    voxels, channels = out_ref.shape
    gather_windows(owner, below_ref, x_ref, above_ref, recv_ref, rim, patch)
    last = recv_ref.shape[1] - 1
    terms = recv_ref[0, last].astype(F32)
    for q in range(1, recv_ref.shape[0]):
        terms = terms + recv_ref[q, last].astype(F32)
    gb_ref[...] = jnp.sum(terms, axis=0, keepdims=True)
    total = jnp.zeros((voxels, channels), F32)
    for dz in range(3):
        for k in range(9):
            total += lax.dot_general(
                patch[8 - k, (2 - dz) * 64 : (2 - dz) * 64 + voxels, :],
                w_ref[dz * 9 + k],
                (((1,), (1,)), ((), ())),
                preferred_element_type=F32,
            )
    out_ref[...] = total.astype(BF)


def unfold_kernel(leaf_units, n_leaves, owner, *refs):
    *pieces, out_ref, flat = refs
    code = leaf_codes(owner.shape[0])
    rel = 0
    for piece in pieces:
        for leaf in range(piece.shape[0] // leaf_units):
            colour = (rel // (n_leaves // 4)) % 2
            row = pl.multiple_of((rel ^ code[colour]) * (leaf_units * ROWS), ROWS)
            block = piece[leaf * leaf_units : (leaf + 1) * leaf_units]
            flat[pl.ds(row, leaf_units * ROWS), :] = block.reshape(-1, 128).astype(F32)
            rel += 1
    pitch = flat.shape[0] // 32
    low = lax.broadcasted_iota(jnp.int32, (8, 128), 1) < 64

    def turned(x):
        return pltpu.roll(x, 64, 1)

    def block(base, group):
        rows = []
        for i in range(2):
            rows.append(
                [
                    flat[pl.ds(base + i + lane * ROWS + group * 8 * pitch, 8, stride=pitch), :]
                    for lane in range(3)
                ]
            )
        (a0, a1, a2), (b0, b1, b2) = rows
        rb0, rb1, ra1, ra2 = turned(b0), turned(b1), turned(a1), turned(a2)
        return (
            a0,
            jnp.where(low, a1, rb0),
            jnp.where(low, rb0, rb1),
            jnp.where(low, ra1, ra2),
            jnp.where(low, ra2, b1),
            b2,
        )

    count = out_ref.shape[0]
    span = out_ref.shape[1] // 2

    def pair(m, carry):
        i = m * 2
        base = (i // ROWS) * (3 * ROWS) + i % ROWS
        for top in range(0, count, 16):
            tiles = [block(base, top // 8), block(base, top // 8 + 1)]
            high = min(16, count - top)
            for n in range(6):
                both = jnp.concatenate([tiles[0][n], tiles[1][n]], axis=0).astype(BF)
                lane = pl.multiple_of((n // 3) * span + m * 384 + (n % 3) * 128, 128)
                out_ref[top : top + high, pl.ds(lane, 128)] = both[:high]
        return carry

    lax.fori_loop(0, span // 384, pair, 0, unroll=8)


def body(features, mask, owner, weight, bias, cotangent):
    channels = bias.shape[0]
    depth = features.shape[0]
    voxels = depth * 64
    regions = lax.axis_size("region")
    tiles = lax.axis_size("batch")
    bits = tiles.bit_length() - 1
    slab = lax.axis_index("region")
    orders = send_orders(tiles)
    n_leaves = 2 * tiles
    units = 27 * (channels // 2 // ROWS) * (2 * channels // 128)
    leaf_units = -(-units // n_leaves)
    barrier = lax.optimization_barrier

    def rims(first, last):
        up = lax.ppermute(last, "region", [(i, i + 1) for i in range(regions - 1)])
        down = lax.ppermute(first, "region", [(i + 1, i) for i in range(regions - 1)])
        return up, down

    def lines_for(below, planes, above, extra):
        return pl.pallas_call(
            lines_kernel,
            out_shape=jax.ShapeDtypeStruct((tiles, depth + 3, EDGE, channels), BF),
            in_specs=[SMEM] + [VMEM] * 4,
            out_specs=VMEM,
            scratch_shapes=[pltpu.VMEM((depth + 2, EDGE, EDGE, channels), F32)],
            compiler_params=PARAMS,
        )(owner, below, planes, above, extra)

    def exchanged(lines):
        return lax.all_to_all(lines, "batch", 0, 0, tiled=True)

    scratch = [
        pltpu.VMEM((depth + 2, 10, 24, channels), F32),
        pltpu.VMEM((9, (depth + 2) * 64, channels), BF),
    ]
    keep = mask.reshape(depth, 64, 1).astype(BF)

    def plane(z):
        return features[z : z + 1].reshape(1, 64, channels) * keep[z : z + 1]

    below, above = rims(plane(0), plane(depth - 1))
    occupied = features.reshape(depth, 64, channels) * keep
    upstream = (cotangent.reshape(depth, 64, channels) * keep).reshape(voxels, channels)
    kernel = weight.reshape(27, channels, channels)
    occupied, kernel, below, above = barrier((occupied, kernel, below, above))
    arrived = exchanged(lines_for(below, occupied, above, jnp.zeros((EDGE, channels), BF)))

    act, grad, bias_terms, terms = pl.pallas_call(
        functools.partial(forward_kernel, leaf_units, n_leaves),
        out_shape=(
            jax.ShapeDtypeStruct((voxels, channels), BF),
            jax.ShapeDtypeStruct((voxels, channels), BF),
            jax.ShapeDtypeStruct((EDGE, channels), BF),
            jax.ShapeDtypeStruct((n_leaves * leaf_units, ROWS, 128), BF),
        ),
        in_specs=[SMEM] + [VMEM] * 7,
        out_specs=(VMEM, VMEM, VMEM, VMEM),
        scratch_shapes=scratch,
        compiler_params=PARAMS,
        cost_estimate=pl.CostEstimate(
            flops=4 * 27 * voxels * channels * channels,
            bytes_accessed=6 << 20,
            transcendentals=voxels * channels,
        ),
    )(owner, below, occupied, above, arrived, kernel, bias.reshape(1, channels), upstream)
    grad = grad.reshape(depth, 64, channels)

    def halve(x, axis, count, flip):
        half = x.shape[0] // 2
        got = lax.ppermute(x[half:].astype(BF), axis, pairs(count, flip))
        return x[:half].astype(F32) + got.astype(F32)

    parts = halve(terms, "batch", tiles, 1)
    split = parts.shape[0] // 2
    colours = [parts[:split], parts[split:]]
    below, above = rims(grad[:1], grad[depth - 1 :])
    for step in range(bits - 1):
        colours = [halve(c, "batch", tiles, 1 << o[step]) for c, o in zip(colours, orders)]
        if step == 0:
            colours, below, above = barrier((colours, below, above))
            lines = lines_for(below, grad, above, bias_terms)
    last = jnp.concatenate(colours, axis=0)
    last, lines = barrier((last, lines))
    arrived = exchanged(lines)
    share = -(-last.shape[0] // regions)
    spare = share * regions - last.shape[0]
    last = jnp.pad(last, ((0, spare), (0, 0), (0, 0))).reshape(regions, share, ROWS, 128)
    flips = sorted(range(1, regions), key=lambda f: -f)
    total = lax.dynamic_index_in_dim(last, slab, 0, False)
    for flip in flips:
        piece = lax.dynamic_index_in_dim(last, slab ^ flip, 0, False).astype(BF)
        total = total + lax.ppermute(piece, "region", pairs(regions, flip)).astype(F32)
    total = total.astype(BF)
    total, arrived = barrier((total, arrived))

    held = [total] + [
        lax.ppermute(total, "region", pairs(regions, flip)) for flip in range(1, regions)
    ]
    whole = jnp.zeros((regions, share, ROWS, 128), BF)
    for flip, block in enumerate(held):
        whole = lax.dynamic_update_index_in_dim(whole, block, slab ^ flip, 0)
    whole = whole.reshape(regions * share, ROWS, 128)

    grad_input, total_bias = pl.pallas_call(
        input_kernel,
        out_shape=(
            jax.ShapeDtypeStruct((voxels, channels), BF),
            jax.ShapeDtypeStruct((1, channels), F32),
        ),
        in_specs=[SMEM] + [VMEM] * 5,
        out_specs=(VMEM, VMEM),
        scratch_shapes=scratch,
        compiler_params=PARAMS,
        cost_estimate=pl.CostEstimate(
            flops=2 * 27 * voxels * channels * channels, bytes_accessed=3 << 20, transcendentals=0
        ),
    )(owner, below, grad, above, arrived, kernel)

    colours = [[whole[:leaf_units]], [whole[leaf_units : 2 * leaf_units]]]
    for step in reversed(range(bits - 1)):
        colours = [
            [jnp.concatenate(c, axis=0) if len(c) > 1 else c[0]] for c in colours
        ]
        colours = [
            c + [lax.ppermute(c[0], "batch", pairs(tiles, 1 << o[step]))]
            for c, o in zip(colours, orders)
        ]
        if step == bits - 2:
            total_bias, grad_input, colours = barrier((total_bias, grad_input, colours))
            for bit in range(regions.bit_length() - 1):
                sent = lax.ppermute(total_bias, "region", pairs(regions, 1 << bit))
                total_bias = total_bias + sent
    near = colours[0] + colours[1]
    far = [lax.ppermute(c, "batch", pairs(tiles, 1)) for c in near]
    kernel_grad = pl.pallas_call(
        functools.partial(unfold_kernel, leaf_units, n_leaves),
        out_shape=jax.ShapeDtypeStruct((27, channels * channels), BF),
        in_specs=[SMEM] + [VMEM] * len(near + far),
        out_specs=VMEM,
        scratch_shapes=[pltpu.VMEM((32 * units // 27 * ROWS, 128), F32)],
        compiler_params=PARAMS,
    )(owner, *near, *far)

    def placed(rows):
        return (rows.reshape(depth, 64, channels) * keep).reshape(features.shape)

    return placed(act), placed(grad_input), kernel_grad, total_bias.reshape(channels)


def solution(mesh):
    split = P("region", "batch", None)
    return jax.shard_map(
        body,
        mesh=mesh,
        in_specs=(split, P("region", "batch"), P(), P(), P(), split),
        out_specs=(split, split, P(), P()),
        check_vma=False,
    )
```

```python
import functools

import jax
import jax.numpy as jnp
from jax import lax
from jax.experimental import pallas as pl
from jax.experimental.pallas import tpu as pltpu
from jax.sharding import PartitionSpec as P

BF = jnp.bfloat16
F32 = jnp.float32
STEPS = ((0, 1), (0, -1), (1, 0), (-1, 0), (1, 1), (1, -1), (-1, 1), (-1, -1))
EDGE = 8
ROWS = 16
VMEM = pl.BlockSpec(memory_space=pltpu.VMEM)
SMEM = pl.BlockSpec(memory_space=pltpu.SMEM)


def vmem(mib):
    return pltpu.CompilerParams(vmem_limit_bytes=mib * 2**20)


def pairs(count, flip):
    return [(i, i ^ flip) for i in range(count)]


def placed_at(owner):
    tiles = owner.shape[0]
    mine = lax.axis_index("batch")
    place = 0
    for q in range(tiles):
        place = place + jnp.where(owner[q] == mine, q, 0)
    return place, tiles // 4, 4


def neighbour(spot, step):
    place, columns, rows = spot
    column = place % columns + step[0]
    row = place // columns + step[1]
    there = (column >= 0) & (column < columns) & (row >= 0) & (row < rows)
    return there, jnp.where(there, place + step[1] * columns + step[0], place)


def leaf_codes(tiles):
    bits = tiles.bit_length() - 1
    mine = lax.axis_index("batch")
    codes = []
    for order in send_orders(tiles):
        code = (mine & 1) << bits
        for n, bit in enumerate(order):
            code = code | (((mine >> bit) & 1) << (bits - 2 - n))
        codes.append(code)
    return codes


def send_orders(tiles):
    bits = tiles.bit_length() - 1
    return tuple(range(1, bits)), tuple(range(bits - 1, 0, -1))


def split_in_three(x):
    terms = []
    for _ in range(3):
        terms.append(x.astype(BF).astype(F32))
        x = x - terms[-1]
    return terms


def unrolled(raw_ref, mask_ref, store):
    count = mask_ref.shape[1]
    wide = raw_ref[...].astype(F32)
    kept = mask_ref[...].astype(F32)
    channels = wide.shape[1] // count
    for y in range(count):
        store(y, wide[:, y * channels : (y + 1) * channels] * kept[:, y : y + 1])


def rolled(rows, mask_ref):
    kept = mask_ref[...].astype(F32)
    parts = [rows[:, y, :] * kept[:, y : y + 1] for y in range(mask_ref.shape[1])]
    return jnp.concatenate(parts, axis=1).astype(BF)


def cut_lines(owner, inner_ref, outer_ref, lines_ref, planes_ref, rim):
    thick, _, _, channels = rim.shape
    odd = lax.axis_index("region") & 1
    for ref, z in ((inner_ref, (thick - 1) * (1 - odd)), (outer_ref, (thick - 1) * odd)):
        planes_ref[z] = ref[0]
        rim[z] = ref[0].reshape(EDGE, EDGE, channels).astype(F32)
    spot = placed_at(owner)
    lines = {
        (0, 1): rim[:, :, 7, :].astype(BF),
        (0, -1): rim[:, :, 0, :].astype(BF),
        (1, 0): rim[:, 7].astype(BF),
        (-1, 0): rim[:, 0].astype(BF),
    }
    for step in STEPS:
        there, place = neighbour(spot, step)
        line = lines[(0, step[1]) if step[1] else step]

        @pl.when(there)
        def _(line=line, place=place):
            lines_ref[owner[place], :thick] = line


def input_lines_kernel(owner, inner_ref, raw_ref, mask_ref, outer_ref, lines_ref, planes_ref, rim):
    depth = rim.shape[0] - 2
    channels = rim.shape[3]

    def store(y, rows):
        rim[1 : depth + 1, :, y, :] = rows.reshape(depth, EDGE, channels)

    unrolled(raw_ref, mask_ref, store)
    planes_ref[1 : depth + 1] = rim[1 : depth + 1].reshape(depth, 64, channels).astype(BF)
    lines_ref[...] = jnp.zeros(lines_ref.shape, BF)
    cut_lines(owner, inner_ref, outer_ref, lines_ref, planes_ref, rim)


def grad_lines_kernel(owner, inner_ref, x_ref, outer_ref, bias_ref, *refs):
    *got_refs, lines_ref, planes_ref, rim = refs
    depth, _, channels = x_ref.shape
    planes_ref[1 : depth + 1] = x_ref[...]
    rim[1 : depth + 1] = x_ref[...].reshape(depth, EDGE, EDGE, channels).astype(F32)
    lines_ref[...] = jnp.zeros(lines_ref.shape, BF)
    terms = bias_ref[0].astype(F32)
    for ref in got_refs:
        terms = terms + ref[ref.shape[0] - 1].astype(F32)
    low = split_in_three(terms[0:1] + terms[2:3] + terms[4:5])
    high = split_in_three(terms[1:2] + terms[3:4] + terms[5:6])
    rows = [jnp.concatenate([a, b[:, : channels - 128]], axis=1) for a, b in zip(low, high)]
    extra = jnp.concatenate(rows + [jnp.zeros((EDGE - 3, channels), F32)], axis=0).astype(BF)
    for q in range(lines_ref.shape[0]):
        lines_ref[q, depth + 2] = extra
    cut_lines(owner, inner_ref, outer_ref, lines_ref, planes_ref, rim)


def gather_windows(owner, x_ref, recv_ref, rim, patch):
    thick, _, channels = x_ref.shape
    rim[:, 1:9, 8:16, :] = x_ref[...].reshape(thick, EDGE, EDGE, channels).astype(F32)
    spot = placed_at(owner)
    lines = [
        recv_ref[owner[neighbour(spot, step)[1]], :thick].astype(F32) for step in STEPS
    ]
    rim[:, 1:9, 16, :] = lines[0]
    rim[:, 1:9, 7, :] = lines[1]
    rim[:, 9, 8:16, :] = lines[2]
    rim[:, 0, 8:16, :] = lines[3]
    rim[:, 9, 16, :] = lines[4][:, 0]
    rim[:, 9, 7, :] = lines[5][:, 0]
    rim[:, 0, 16, :] = lines[6][:, 7]
    rim[:, 0, 7, :] = lines[7][:, 7]

    def plane(z, carry):
        for dx in range(3):
            for dy in range(3):
                seen = rim[z, dx : dx + 8, 7 + dy : 15 + dy, :]
                row = pl.multiple_of(z * 64, 64)
                patch[dx * 3 + dy, pl.ds(row, 64), :] = seen.reshape(64, channels).astype(BF)
        return carry

    lax.fori_loop(0, thick, plane, 0)


def forward_kernel(share, regions, n_leaves, owner, x_ref, recv_ref, w_ref, bias_ref,
                   cot_ref, mask_ref, act_ref, gp_ref, gb_ref, gw_ref, rim, patch, cot):
    voxels, channels = gp_ref.shape

    def store(y, rows):
        cot[:, y, :] = rows

    unrolled(cot_ref, mask_ref, store)
    gather_windows(owner, x_ref, recv_ref, rim, patch)
    pre = jnp.broadcast_to(bias_ref[...], (voxels, channels))
    for dz in range(3):
        for k in range(9):
            pre += jnp.dot(
                patch[k, dz * 64 : dz * 64 + voxels, :],
                w_ref[dz * 9 + k],
                preferred_element_type=F32,
            )
    sigma = jax.nn.sigmoid(pre)
    upstream = cot[...].reshape(voxels, channels)
    grad = (upstream * sigma * (1.0 + pre * (1.0 - sigma))).astype(BF)
    gp_ref[...] = grad
    cot[...] = (pre * sigma).reshape(cot.shape)
    act_ref[...] = rolled(cot, mask_ref)
    rest = jnp.sum(grad.astype(F32), axis=0, keepdims=True)
    rows = []
    for term in split_in_three(rest):
        tail = jnp.zeros((1, 256 - channels), F32)
        rows += [term[:, :128], jnp.concatenate([term[:, 128:], tail], axis=1)]
    rows.append(jnp.zeros((ROWS - len(rows), 128), F32))
    gb_ref[0] = jnp.concatenate(rows, axis=0).astype(BF)
    half = channels // 2
    per_offset = half // ROWS
    lanes = 2 * channels // 128
    code = leaf_codes(owner.shape[0])

    slab = lax.axis_index("region")

    def put(unit, value):
        part, inner = divmod(unit, share)
        leaf, level = divmod(part, regions)
        colour = (leaf // (n_leaves // 4)) % 2
        gw_ref[((leaf ^ code[colour]) * regions + (level ^ slab)) * share + inner] = value

    for dz in range(3):
        for k in range(9):
            o = dz * 9 + k
            part = lax.dot_general(
                patch[k, dz * 64 : dz * 64 + voxels, :],
                grad,
                (((0,), (0,)), ((), ())),
                preferred_element_type=F32,
            )
            wide = jnp.concatenate([part[:half], part[half:]], axis=1).astype(BF)
            for rows in range(per_offset):
                for lane in range(lanes):
                    put(
                        (o * per_offset + rows) * lanes + lane,
                        wide[rows * ROWS : (rows + 1) * ROWS, lane * 128 : (lane + 1) * 128],
                    )
    for unit in range(27 * per_offset * lanes, share * regions * n_leaves):
        put(unit, jnp.zeros((ROWS, 128), BF))


def input_kernel(owner, x_ref, recv_ref, w_ref, mask_ref, out_ref, gb_ref, rim, patch, rows):
    channels = w_ref.shape[1]
    voxels = (x_ref.shape[0] - 2) * 64
    gather_windows(owner, x_ref, recv_ref, rim, patch)
    last = recv_ref.shape[1] - 1
    terms = recv_ref[0, last].astype(F32)
    for q in range(1, recv_ref.shape[0]):
        terms = terms + recv_ref[q, last].astype(F32)
    gb_ref[...] = jnp.sum(terms, axis=0, keepdims=True)
    total = jnp.zeros((voxels, channels), F32)
    for dz in range(3):
        for k in range(9):
            total += lax.dot_general(
                patch[8 - k, (2 - dz) * 64 : (2 - dz) * 64 + voxels, :],
                w_ref[dz * 9 + k],
                (((1,), (1,)), ((), ())),
                preferred_element_type=F32,
            )
    rows[...] = total.reshape(rows.shape)
    out_ref[...] = rolled(rows, mask_ref)


def unfold_kernel(share, regions, n_leaves, owner, *refs):
    *pieces, out_ref, flat = refs
    code = leaf_codes(owner.shape[0])
    slab = lax.axis_index("region")
    part = 0
    for piece in pieces:
        for first in range(0, piece.shape[0], share):
            rel, level = divmod(part, regions)
            colour = (rel // (n_leaves // 4)) % 2
            row = ((rel ^ code[colour]) * regions + (level ^ slab)) * (share * ROWS)
            block = piece[first : first + share]
            flat[pl.ds(pl.multiple_of(row, ROWS), share * ROWS), :] = block.reshape(
                share * ROWS, 128
            ).astype(F32)
            part += 1
    pitch = out_ref.shape[1] // 128
    low = lax.broadcasted_iota(jnp.int32, (8, 128), 1) < 64

    def turned(x):
        return pltpu.roll(x, 64, 1)

    def block(base, group):
        rows = []
        for i in range(2):
            rows.append(
                [
                    flat[pl.ds(base + i + lane * ROWS + group * 8 * pitch, 8, stride=pitch), :]
                    for lane in range(3)
                ]
            )
        (a0, a1, a2), (b0, b1, b2) = rows
        rb0, rb1, ra1, ra2 = turned(b0), turned(b1), turned(a1), turned(a2)
        return (
            a0,
            jnp.where(low, a1, rb0),
            jnp.where(low, rb0, rb1),
            jnp.where(low, ra1, ra2),
            jnp.where(low, ra2, b1),
            b2,
        )

    count = out_ref.shape[0]
    span = out_ref.shape[1] // 2

    def pair(m, carry):
        i = m * 2
        base = (i // ROWS) * (3 * ROWS) + i % ROWS
        for top in range(0, count, 16):
            tiles = [block(base, top // 8), block(base, top // 8 + 1)]
            high = min(16, count - top)
            for n in range(6):
                both = jnp.concatenate([tiles[0][n], tiles[1][n]], axis=0).astype(BF)
                lane = pl.multiple_of((n // 3) * span + m * 384 + (n % 3) * 128, 128)
                out_ref[top : top + high, pl.ds(lane, 128)] = both[:high]
        return carry

    lax.fori_loop(0, span // 384, pair, 0, unroll=8)


def body(features, mask, owner, weight, bias, cotangent):
    channels = bias.shape[0]
    depth = features.shape[0]
    voxels = depth * 64
    regions = lax.axis_size("region")
    tiles = lax.axis_size("batch")
    bits = tiles.bit_length() - 1
    slab = lax.axis_index("region")
    orders = send_orders(tiles)
    n_leaves = 2 * tiles
    units = 27 * (channels // 2 // ROWS) * (2 * channels // 128)
    leaf_units = -(-units // (n_leaves * regions)) * regions
    share = leaf_units // regions
    barrier = lax.optimization_barrier

    odd = slab & 1
    joined = [[(i, i ^ 1) for i in range(regions)]]
    joined.append([(i, i + 1 - 2 * (1 - i % 2)) for i in range(1, regions - 1)])

    def rims(plane):
        top = depth - 1
        inner = lax.ppermute(plane(top * (1 - odd)), "region", joined[0])
        outer = lax.ppermute(plane(top * odd), "region", joined[1])
        return inner, outer

    def cut(kernel, extra_planes, operands):
        return pl.pallas_call(
            kernel,
            out_shape=(
                jax.ShapeDtypeStruct((tiles, depth + 2 + extra_planes, EDGE, channels), BF),
                jax.ShapeDtypeStruct((depth + 2, 64, channels), BF),
            ),
            in_specs=[SMEM] + [VMEM] * len(operands),
            out_specs=(VMEM, VMEM),
            scratch_shapes=[pltpu.VMEM((depth + 2, EDGE, EDGE, channels), F32)],
            compiler_params=vmem(12),
        )(owner, *operands)

    def exchanged(lines):
        return lax.all_to_all(lines, "batch", 0, 0, tiled=True)

    scratch = [
        pltpu.VMEM((depth + 2, 10, 24, channels), F32),
        pltpu.VMEM((9, (depth + 2) * 64, channels), BF),
        pltpu.VMEM((depth * EDGE, EDGE, channels), F32),
    ]
    marks = mask.reshape(depth * EDGE, EDGE)
    flat = (depth * EDGE, EDGE * channels)

    def own_plane(z):
        seen = lax.dynamic_slice_in_dim(features, z, 1, 0).reshape(1, 64, channels)
        kept = lax.dynamic_slice_in_dim(mask, z, 1, 0).reshape(1, 64, 1)
        return seen * kept.astype(BF)

    inner, outer = rims(own_plane)
    lines, planes = cut(input_lines_kernel, 0, (inner, features.reshape(flat), marks, outer))
    lines, weight = barrier((lines, weight))
    arrived = exchanged(lines)
    kernel = weight.reshape(27, channels, channels)

    act, grad, bias_terms, terms = pl.pallas_call(
        functools.partial(forward_kernel, share, regions, n_leaves),
        out_shape=(
            jax.ShapeDtypeStruct(flat, BF),
            jax.ShapeDtypeStruct((voxels, channels), BF),
            jax.ShapeDtypeStruct((1, ROWS, 128), BF),
            jax.ShapeDtypeStruct((n_leaves * leaf_units, ROWS, 128), BF),
        ),
        in_specs=[SMEM] + [VMEM] * 6,
        out_specs=(VMEM, VMEM, VMEM, VMEM),
        scratch_shapes=scratch,
        compiler_params=vmem(24),
        cost_estimate=pl.CostEstimate(
            flops=4 * 27 * voxels * channels * channels,
            bytes_accessed=6 << 20,
            transcendentals=voxels * channels,
        ),
    )(owner, planes, arrived, kernel, bias.reshape(1, channels), cotangent.reshape(flat), marks)
    grad = grad.reshape(depth, 64, channels)

    def halve(x, axis, count, flip):
        half = x.shape[0] // 2
        got = lax.ppermute(x[half:].astype(BF), axis, pairs(count, flip))
        return x[:half].astype(F32) + got.astype(F32)

    parts = halve(terms, "batch", tiles, 1)
    split = parts.shape[0] // 2
    colours = [parts[:split], parts[split:]]
    inner, outer = rims(lambda z: lax.dynamic_slice_in_dim(grad, z, 1, 0))
    for step in range(bits - 1):
        colours = [halve(c, "batch", tiles, 1 << o[step]) for c, o in zip(colours, orders)]
        if step == 0:
            colours, inner, outer = barrier((colours, inner, outer))

    def level(k):
        return [c[k * share : (k + 1) * share] for c in colours]

    total = jnp.concatenate(level(0), axis=0)
    gots = []
    for flip in sorted(range(1, regions), key=lambda f: -f):
        sent = jnp.concatenate([x.astype(BF) for x in level(flip)] + [bias_terms], axis=0)
        gots.append(lax.ppermute(sent, "region", pairs(regions, flip)))
        total = total + gots[-1][:-1].astype(F32)
    total = total.astype(BF)
    lines, grad_planes = cut(grad_lines_kernel, 1, (inner, grad, outer, bias_terms, *gots))
    arrived = exchanged(lines)

    held = [total] + [
        lax.ppermute(total, "region", pairs(regions, flip)) for flip in range(1, regions)
    ]
    grad_input, total_bias = pl.pallas_call(
        input_kernel,
        out_shape=(
            jax.ShapeDtypeStruct(flat, BF),
            jax.ShapeDtypeStruct((1, channels), F32),
        ),
        in_specs=[SMEM] + [VMEM] * 4,
        out_specs=(VMEM, VMEM),
        scratch_shapes=scratch,
        compiler_params=vmem(20),
        cost_estimate=pl.CostEstimate(
            flops=2 * 27 * voxels * channels * channels, bytes_accessed=3 << 20, transcendentals=0
        ),
    )(owner, grad_planes, arrived, kernel, marks)

    colours = [
        [jnp.concatenate([h[c * share : (c + 1) * share] for h in held], axis=0)] for c in range(2)
    ]
    for step in reversed(range(bits - 1)):
        colours = [
            c + [lax.ppermute(x, "batch", pairs(tiles, 1 << o[step])) for x in c]
            for c, o in zip(colours, orders)
        ]
        if step == bits - 2:
            first = [c[1] for c in colours]
            first, grad_input = barrier((first, grad_input))
            colours = [[c[0], f] for c, f in zip(colours, first)]
    near = colours[0] + colours[1]
    far = [lax.ppermute(c, "batch", pairs(tiles, 1)) for c in near]
    kernel_grad = pl.pallas_call(
        functools.partial(unfold_kernel, share, regions, n_leaves),
        out_shape=jax.ShapeDtypeStruct((27, channels * channels), BF),
        in_specs=[SMEM] + [VMEM] * len(near + far),
        out_specs=VMEM,
        scratch_shapes=[pltpu.VMEM((max(32 * units // 27, n_leaves * leaf_units) * ROWS, 128), F32)],
        compiler_params=vmem(20),
    )(owner, *near, *far)

    shape = features.shape
    return act.reshape(shape), grad_input.reshape(shape), kernel_grad, total_bias.reshape(channels)


def solution(mesh):
    split = P("region", "batch", None)
    return jax.shard_map(
        body,
        mesh=mesh,
        in_specs=(split, P("region", "batch"), P(), P(), P(), split),
        out_specs=(split, split, P(), P()),
        check_vma=False,
    )
```

```python
import functools

import jax
import jax.numpy as jnp
from jax import lax
from jax.experimental import pallas as pl
from jax.experimental.pallas import tpu as pltpu
from jax.sharding import PartitionSpec as P

BF = jnp.bfloat16
F32 = jnp.float32
STEPS = ((0, 1), (0, -1), (1, 0), (-1, 0), (1, 1), (1, -1), (-1, 1), (-1, -1))
EDGE = 8
ROWS = 16
PITCH = 17
VMEM = pl.BlockSpec(memory_space=pltpu.VMEM)
SMEM = pl.BlockSpec(memory_space=pltpu.SMEM)


def vmem(mib):
    return pltpu.CompilerParams(vmem_limit_bytes=mib * 2**20)


def pairs(count, flip):
    return [(i, i ^ flip) for i in range(count)]


def placed_at(owner):
    tiles = owner.shape[0]
    mine = lax.axis_index("batch")
    place = 0
    for q in range(tiles):
        place = place + jnp.where(owner[q] == mine, q, 0)
    return place, tiles // 4, 4


def neighbour(spot, step):
    place, columns, rows = spot
    column = place % columns + step[0]
    row = place // columns + step[1]
    there = (column >= 0) & (column < columns) & (row >= 0) & (row < rows)
    return there, jnp.where(there, place + step[1] * columns + step[0], place)


def leaf_codes(tiles):
    bits = tiles.bit_length() - 1
    mine = lax.axis_index("batch")
    codes = []
    for order in send_orders(tiles):
        code = (mine & 1) << bits
        for n, bit in enumerate(order):
            code = code | (((mine >> bit) & 1) << (bits - 2 - n))
        codes.append(code)
    return codes


def send_orders(tiles):
    bits = tiles.bit_length() - 1
    return tuple(range(1, bits)), tuple(range(bits - 1, 0, -1))


def split_in_three(x):
    terms = []
    for _ in range(3):
        terms.append(x.astype(BF).astype(F32))
        x = x - terms[-1]
    return terms


def unrolled(raw_ref, mask_ref, store):
    count = mask_ref.shape[1]
    wide = raw_ref[...].astype(F32)
    kept = mask_ref[...].astype(F32)
    channels = wide.shape[1] // count
    for y in range(count):
        store(y, wide[:, y * channels : (y + 1) * channels] * kept[:, y : y + 1])


def rolled(rows, mask_ref):
    kept = mask_ref[...].astype(F32)
    parts = [rows[:, y, :] * kept[:, y : y + 1] for y in range(mask_ref.shape[1])]
    return jnp.concatenate(parts, axis=1).astype(BF)


def cut_lines(owner, inner_ref, outer_ref, lines_ref, planes_ref, rim):
    thick, _, _, channels = rim.shape
    odd = lax.axis_index("region") & 1
    for ref, z in ((inner_ref, (thick - 1) * (1 - odd)), (outer_ref, (thick - 1) * odd)):
        planes_ref[z] = ref[0]
        rim[z] = ref[0].reshape(EDGE, EDGE, channels).astype(F32)
    spot = placed_at(owner)
    lines = {
        (0, 1): rim[:, :, 7, :].astype(BF),
        (0, -1): rim[:, :, 0, :].astype(BF),
        (1, 0): rim[:, 7].astype(BF),
        (-1, 0): rim[:, 0].astype(BF),
    }
    for step in STEPS:
        there, place = neighbour(spot, step)
        line = lines[(0, step[1]) if step[1] else step]

        @pl.when(there)
        def _(line=line, place=place):
            lines_ref[owner[place], :thick] = line


def occupied_kernel(owner, raw_ref, mask_ref, out_ref, rows_ref):
    def store(y, rows):
        rows_ref[:, y, :] = rows

    unrolled(raw_ref, mask_ref, store)
    out_ref[...] = rows_ref[...].reshape(out_ref.shape).astype(BF)


def fill_planes(x_ref, planes_ref, lines_ref, rim):
    depth, _, channels = x_ref.shape
    planes_ref[1 : depth + 1] = x_ref[...]
    rim[1 : depth + 1] = x_ref[...].reshape(depth, EDGE, EDGE, channels).astype(F32)
    lines_ref[...] = jnp.zeros(lines_ref.shape, BF)


def input_lines_kernel(owner, inner_ref, x_ref, outer_ref, lines_ref, planes_ref, rim):
    fill_planes(x_ref, planes_ref, lines_ref, rim)
    cut_lines(owner, inner_ref, outer_ref, lines_ref, planes_ref, rim)


def grad_lines_kernel(owner, inner_ref, x_ref, outer_ref, bias_ref, *refs):
    *got_refs, lines_ref, planes_ref, rim = refs
    depth, _, channels = x_ref.shape
    fill_planes(x_ref, planes_ref, lines_ref, rim)
    terms = bias_ref[0].astype(F32)
    for ref in got_refs:
        terms = terms + ref[ref.shape[0] - 1].astype(F32)
    low = split_in_three(terms[0:1] + terms[2:3] + terms[4:5])
    high = split_in_three(terms[1:2] + terms[3:4] + terms[5:6])
    rows = [jnp.concatenate([a, b[:, : channels - 128]], axis=1) for a, b in zip(low, high)]
    extra = jnp.concatenate(rows + [jnp.zeros((EDGE - 3, channels), F32)], axis=0).astype(BF)
    for q in range(lines_ref.shape[0]):
        lines_ref[q, depth + 2] = extra
    cut_lines(owner, inner_ref, outer_ref, lines_ref, planes_ref, rim)


def gather_windows(owner, x_ref, recv_ref, rim, patch):
    thick, _, channels = x_ref.shape
    rim[:, 1:9, 8:16, :] = x_ref[...].reshape(thick, EDGE, EDGE, channels).astype(F32)
    spot = placed_at(owner)
    lines = [
        recv_ref[owner[neighbour(spot, step)[1]], :thick].astype(F32) for step in STEPS
    ]
    rim[:, 1:9, 16, :] = lines[0]
    rim[:, 1:9, 7, :] = lines[1]
    rim[:, 9, 8:16, :] = lines[2]
    rim[:, 0, 8:16, :] = lines[3]
    rim[:, 9, 16, :] = lines[4][:, 0]
    rim[:, 9, 7, :] = lines[5][:, 0]
    rim[:, 0, 16, :] = lines[6][:, 7]
    rim[:, 0, 7, :] = lines[7][:, 7]

    def plane(z, carry):
        for dx in range(3):
            for dy in range(3):
                seen = rim[z, dx : dx + 8, 7 + dy : 15 + dy, :]
                row = pl.multiple_of(z * 64, 64)
                patch[dx * 3 + dy, pl.ds(row, 64), :] = seen.reshape(64, channels).astype(BF)
        return carry

    lax.fori_loop(0, thick, plane, 0)


def forward_kernel(share, regions, n_leaves, owner, x_ref, recv_ref, w_ref, bias_ref,
                   cot_ref, mask_ref, act_ref, gp_ref, gb_ref, gw_ref, rim, patch, cot):
    voxels, channels = gp_ref.shape

    def store(y, rows):
        cot[:, y, :] = rows

    unrolled(cot_ref, mask_ref, store)
    gather_windows(owner, x_ref, recv_ref, rim, patch)
    pre = jnp.broadcast_to(bias_ref[...], (voxels, channels))
    for dz in range(3):
        for k in range(9):
            pre += jnp.dot(
                patch[k, dz * 64 : dz * 64 + voxels, :],
                w_ref[dz * 9 + k],
                preferred_element_type=F32,
            )
    sigma = jax.nn.sigmoid(pre)
    upstream = cot[...].reshape(voxels, channels)
    grad = (upstream * sigma * (1.0 + pre * (1.0 - sigma))).astype(BF)
    gp_ref[...] = grad
    act_ref[...] = (pre * sigma).astype(BF)
    rest = jnp.sum(grad.astype(F32), axis=0, keepdims=True)
    rows = []
    for term in split_in_three(rest):
        tail = jnp.zeros((1, 256 - channels), F32)
        rows += [term[:, :128], jnp.concatenate([term[:, 128:], tail], axis=1)]
    rows.append(jnp.zeros((ROWS - len(rows), 128), F32))
    gb_ref[0] = jnp.concatenate(rows, axis=0).astype(BF)
    half = channels // 2
    per_offset = half // ROWS
    lanes = 2 * channels // 128
    code = leaf_codes(owner.shape[0])

    slab = lax.axis_index("region")

    def put(unit, value):
        part, inner = divmod(unit, share)
        leaf, level = divmod(part, regions)
        colour = (leaf // (n_leaves // 4)) % 2
        gw_ref[((leaf ^ code[colour]) * regions + (level ^ slab)) * share + inner] = value

    for dz in range(3):
        for k in range(9):
            o = dz * 9 + k
            part = lax.dot_general(
                patch[k, dz * 64 : dz * 64 + voxels, :],
                grad,
                (((0,), (0,)), ((), ())),
                preferred_element_type=F32,
            )
            wide = jnp.concatenate([part[:half], part[half:]], axis=1).astype(BF)
            for rows in range(per_offset):
                for lane in range(lanes):
                    put(
                        (o * per_offset + rows) * lanes + lane,
                        wide[rows * ROWS : (rows + 1) * ROWS, lane * 128 : (lane + 1) * 128],
                    )
    for unit in range(27 * per_offset * lanes, share * regions * n_leaves):
        put(unit, jnp.zeros((ROWS, 128), BF))


def input_kernel(owner, x_ref, recv_ref, w_ref, mask_ref, pre_ref, out_ref, act_ref, gb_ref,
                 rim, patch, rows):
    channels = w_ref.shape[1]
    voxels = (x_ref.shape[0] - 2) * 64
    gather_windows(owner, x_ref, recv_ref, rim, patch)
    last = recv_ref.shape[1] - 1
    terms = recv_ref[0, last].astype(F32)
    for q in range(1, recv_ref.shape[0]):
        terms = terms + recv_ref[q, last].astype(F32)
    gb_ref[...] = jnp.sum(terms, axis=0, keepdims=True)
    total = jnp.zeros((voxels, channels), F32)
    for dz in range(3):
        for k in range(9):
            total += lax.dot_general(
                patch[8 - k, (2 - dz) * 64 : (2 - dz) * 64 + voxels, :],
                w_ref[dz * 9 + k],
                (((1,), (1,)), ((), ())),
                preferred_element_type=F32,
            )
    rows[...] = pre_ref[...].astype(F32).reshape(rows.shape)
    act_ref[...] = rolled(rows, mask_ref)
    rows[...] = total.reshape(rows.shape)
    out_ref[...] = rolled(rows, mask_ref)


def unfold_kernel(share, regions, n_leaves, owner, *refs):
    *pieces, out_ref, flat = refs
    code = leaf_codes(owner.shape[0])
    slab = lax.axis_index("region")
    part = 0
    for piece in pieces:
        for first in range(0, piece.shape[0], share):
            rel, level = divmod(part, regions)
            colour = (rel // (n_leaves // 4)) % 2
            row = ((rel ^ code[colour]) * regions + (level ^ slab)) * (share * PITCH)
            for n in range(share):
                flat[pl.ds(row + n * PITCH, ROWS), :] = piece[first + n].astype(F32)
            part += 1
    pitch = out_ref.shape[1] // (128 * ROWS) * PITCH
    low = lax.broadcasted_iota(jnp.int32, (8, 128), 1) < 64

    def turned(x):
        return pltpu.roll(x, 64, 1)

    def block(base, group):
        rows = []
        for i in range(2):
            rows.append(
                [
                    flat[pl.ds(base + i + lane * PITCH + group * 8 * pitch, 8, stride=pitch), :]
                    for lane in range(3)
                ]
            )
        (a0, a1, a2), (b0, b1, b2) = rows
        rb0, rb1, ra1, ra2 = turned(b0), turned(b1), turned(a1), turned(a2)
        return (
            a0,
            jnp.where(low, a1, rb0),
            jnp.where(low, rb0, rb1),
            jnp.where(low, ra1, ra2),
            jnp.where(low, ra2, b1),
            b2,
        )

    count = out_ref.shape[0]
    span = out_ref.shape[1] // 2

    def pair(m, carry):
        i = m * 2
        base = (i // ROWS) * (3 * PITCH) + i % ROWS
        for top in range(0, count, 16):
            tiles = [block(base, top // 8), block(base, top // 8 + 1)]
            high = min(16, count - top)
            for n in range(6):
                both = jnp.concatenate([tiles[0][n], tiles[1][n]], axis=0).astype(BF)
                lane = pl.multiple_of((n // 3) * span + m * 384 + (n % 3) * 128, 128)
                out_ref[top : top + high, pl.ds(lane, 128)] = both[:high]
        return carry

    lax.fori_loop(0, span // 384, pair, 0, unroll=8)


def body(features, mask, owner, weight, bias, cotangent):
    channels = bias.shape[0]
    depth = features.shape[0]
    voxels = depth * 64
    regions = lax.axis_size("region")
    tiles = lax.axis_size("batch")
    bits = tiles.bit_length() - 1
    slab = lax.axis_index("region")
    orders = send_orders(tiles)
    n_leaves = 2 * tiles
    units = 27 * (channels // 2 // ROWS) * (2 * channels // 128)
    leaf_units = -(-units // (n_leaves * regions)) * regions
    share = leaf_units // regions
    barrier = lax.optimization_barrier

    odd = slab & 1
    joined = [[(i, i ^ 1) for i in range(regions)]]
    joined.append([(i, i + 1 - 2 * (1 - i % 2)) for i in range(1, regions - 1)])

    def rims(plane):
        top = depth - 1
        inner = lax.ppermute(plane(top * (1 - odd)), "region", joined[0])
        outer = lax.ppermute(plane(top * odd), "region", joined[1])
        return inner, outer

    def cut(kernel, extra_planes, operands):
        return pl.pallas_call(
            kernel,
            out_shape=(
                jax.ShapeDtypeStruct((tiles, depth + 2 + extra_planes, EDGE, channels), BF),
                jax.ShapeDtypeStruct((depth + 2, 64, channels), BF),
            ),
            in_specs=[SMEM] + [VMEM] * len(operands),
            out_specs=(VMEM, VMEM),
            scratch_shapes=[pltpu.VMEM((depth + 2, EDGE, EDGE, channels), F32)],
            compiler_params=vmem(12),
        )(owner, *operands)

    def exchanged(lines):
        return lax.all_to_all(lines, "batch", 0, 0, tiled=True)

    scratch = [
        pltpu.VMEM((depth + 2, 10, 24, channels), F32),
        pltpu.VMEM((9, (depth + 2) * 64, channels), BF),
        pltpu.VMEM((depth * EDGE, EDGE, channels), F32),
    ]
    marks = mask.reshape(depth * EDGE, EDGE)
    flat = (depth * EDGE, EDGE * channels)

    def own_plane(z):
        seen = lax.dynamic_slice_in_dim(features, z, 1, 0).reshape(1, 64, channels)
        kept = lax.dynamic_slice_in_dim(mask, z, 1, 0).reshape(1, 64, 1)
        return seen * kept.astype(BF)

    inner, outer = rims(own_plane)
    occupied = pl.pallas_call(
        occupied_kernel,
        out_shape=jax.ShapeDtypeStruct((depth, 64, channels), BF),
        in_specs=[SMEM, VMEM, VMEM],
        out_specs=VMEM,
        scratch_shapes=[pltpu.VMEM((depth * EDGE, EDGE, channels), F32)],
        compiler_params=vmem(12),
    )(owner, features.reshape(flat), marks)
    lines, planes = cut(input_lines_kernel, 0, (inner, occupied, outer))
    lines, weight = barrier((lines, weight))
    arrived = exchanged(lines)
    kernel = weight.reshape(27, channels, channels)

    act, grad, bias_terms, terms = pl.pallas_call(
        functools.partial(forward_kernel, share, regions, n_leaves),
        out_shape=(
            jax.ShapeDtypeStruct((voxels, channels), BF),
            jax.ShapeDtypeStruct((voxels, channels), BF),
            jax.ShapeDtypeStruct((1, ROWS, 128), BF),
            jax.ShapeDtypeStruct((n_leaves * leaf_units, ROWS, 128), BF),
        ),
        in_specs=[SMEM] + [VMEM] * 6,
        out_specs=(VMEM, VMEM, VMEM, VMEM),
        scratch_shapes=scratch,
        compiler_params=vmem(24),
        cost_estimate=pl.CostEstimate(
            flops=4 * 27 * voxels * channels * channels,
            bytes_accessed=6 << 20,
            transcendentals=voxels * channels,
        ),
    )(owner, planes, arrived, kernel, bias.reshape(1, channels), cotangent.reshape(flat), marks)
    grad = grad.reshape(depth, 64, channels)

    def halve(x, axis, count, flip):
        half = x.shape[0] // 2
        got = lax.ppermute(x[half:].astype(BF), axis, pairs(count, flip))
        return x[:half].astype(F32) + got.astype(F32)

    parts = halve(terms, "batch", tiles, 1)
    split = parts.shape[0] // 2
    colours = [parts[:split], parts[split:]]
    inner, outer = rims(lambda z: lax.dynamic_slice_in_dim(grad, z, 1, 0))
    for step in range(bits - 1):
        colours = [halve(c, "batch", tiles, 1 << o[step]) for c, o in zip(colours, orders)]
        if step == 0:
            colours, inner, outer = barrier((colours, inner, outer))

    def level(k):
        return [c[k * share : (k + 1) * share] for c in colours]

    total = jnp.concatenate(level(0), axis=0)
    gots = []
    for flip in sorted(range(1, regions), key=lambda f: -f):
        sent = jnp.concatenate([x.astype(BF) for x in level(flip)] + [bias_terms], axis=0)
        gots.append(lax.ppermute(sent, "region", pairs(regions, flip)))
        total = total + gots[-1][:-1].astype(F32)
    total = total.astype(BF)
    lines, grad_planes = cut(grad_lines_kernel, 1, (inner, grad, outer, bias_terms, *gots))
    arrived = exchanged(lines)

    held = [total] + [
        lax.ppermute(total, "region", pairs(regions, flip)) for flip in range(1, regions)
    ]
    grad_input, activation, total_bias = pl.pallas_call(
        input_kernel,
        out_shape=(
            jax.ShapeDtypeStruct(flat, BF),
            jax.ShapeDtypeStruct(flat, BF),
            jax.ShapeDtypeStruct((1, channels), F32),
        ),
        in_specs=[SMEM] + [VMEM] * 5,
        out_specs=(VMEM, VMEM, VMEM),
        scratch_shapes=scratch,
        compiler_params=vmem(20),
        cost_estimate=pl.CostEstimate(
            flops=2 * 27 * voxels * channels * channels, bytes_accessed=3 << 20, transcendentals=0
        ),
    )(owner, grad_planes, arrived, kernel, marks, act)

    colours = [
        [jnp.concatenate([h[c * share : (c + 1) * share] for h in held], axis=0)] for c in range(2)
    ]
    for step in reversed(range(bits - 1)):
        colours = [
            c + [lax.ppermute(x, "batch", pairs(tiles, 1 << o[step])) for x in c]
            for c, o in zip(colours, orders)
        ]
        if step == bits - 2:
            first = [c[1] for c in colours]
            first, grad_input = barrier((first, grad_input))
            colours = [[c[0], f] for c, f in zip(colours, first)]
    near = colours[0] + colours[1]
    far = [lax.ppermute(c, "batch", pairs(tiles, 1)) for c in near]
    kernel_grad = pl.pallas_call(
        functools.partial(unfold_kernel, share, regions, n_leaves),
        out_shape=jax.ShapeDtypeStruct((27, channels * channels), BF),
        in_specs=[SMEM] + [VMEM] * len(near + far),
        out_specs=VMEM,
        scratch_shapes=[pltpu.VMEM((max(32 * units // 27, n_leaves * leaf_units) * PITCH, 128), F32)],
        compiler_params=vmem(20),
    )(owner, *near, *far)

    shape = features.shape
    outs = activation.reshape(shape), grad_input.reshape(shape)
    return *outs, kernel_grad, total_bias.reshape(channels)


def solution(mesh):
    split = P("region", "batch", None)
    return jax.shard_map(
        body,
        mesh=mesh,
        in_specs=(split, P("region", "batch"), P(), P(), P(), split),
        out_specs=(split, split, P(), P()),
        check_vma=False,
    )
```

```python
import functools

import jax
import jax.numpy as jnp
from jax import lax
from jax.experimental import pallas as pl
from jax.experimental.pallas import tpu as pltpu
from jax.sharding import PartitionSpec as P

BF = jnp.bfloat16
F32 = jnp.float32
STEPS = ((0, 1), (0, -1), (1, 0), (-1, 0), (1, 1), (1, -1), (-1, 1), (-1, -1))
EDGE = 8
ROWS = 16
PITCH = 17
VMEM = pl.BlockSpec(memory_space=pltpu.VMEM)
SMEM = pl.BlockSpec(memory_space=pltpu.SMEM)


def vmem(mib):
    return pltpu.CompilerParams(vmem_limit_bytes=mib * 2**20)


def pairs(count, flip):
    return [(i, i ^ flip) for i in range(count)]


def placed_at(owner):
    tiles = owner.shape[0]
    mine = lax.axis_index("batch")
    place = 0
    for q in range(tiles):
        place = place + jnp.where(owner[q] == mine, q, 0)
    return place, tiles // 4, 4


def neighbour(spot, step):
    place, columns, rows = spot
    column = place % columns + step[0]
    row = place // columns + step[1]
    there = (column >= 0) & (column < columns) & (row >= 0) & (row < rows)
    return there, jnp.where(there, place + step[1] * columns + step[0], place)


def leaf_codes(tiles):
    bits = tiles.bit_length() - 1
    mine = lax.axis_index("batch")
    codes = []
    for order in send_orders(tiles):
        code = (mine & 1) << bits
        for n, bit in enumerate(order):
            code = code | (((mine >> bit) & 1) << (bits - 2 - n))
        codes.append(code)
    return codes


def send_orders(tiles):
    bits = tiles.bit_length() - 1
    return tuple(range(1, bits)), tuple(range(bits - 1, 0, -1))


def split_in_three(x):
    terms = []
    for _ in range(3):
        terms.append(x.astype(BF).astype(F32))
        x = x - terms[-1]
    return terms


def unrolled(raw_ref, mask_ref, store):
    count = mask_ref.shape[1]
    wide = raw_ref[...].astype(F32)
    kept = mask_ref[...].astype(F32)
    channels = wide.shape[1] // count
    for y in range(count):
        store(y, wide[:, y * channels : (y + 1) * channels] * kept[:, y : y + 1])


def rolled(rows, mask_ref):
    kept = mask_ref[...].astype(F32)
    parts = [rows[:, y, :] * kept[:, y : y + 1] for y in range(mask_ref.shape[1])]
    return jnp.concatenate(parts, axis=1).astype(BF)


def cut_lines(owner, inner_ref, outer_ref, lines_ref, planes_ref, rim):
    thick, _, _, channels = rim.shape
    odd = lax.axis_index("region") & 1
    for ref, z in ((inner_ref, (thick - 1) * (1 - odd)), (outer_ref, (thick - 1) * odd)):
        planes_ref[z] = ref[0]
        rim[z] = ref[0].reshape(EDGE, EDGE, channels).astype(F32)
    spot = placed_at(owner)
    lines = {
        (0, 1): rim[:, :, 7, :].astype(BF),
        (0, -1): rim[:, :, 0, :].astype(BF),
        (1, 0): rim[:, 7].astype(BF),
        (-1, 0): rim[:, 0].astype(BF),
    }
    for step in STEPS:
        there, place = neighbour(spot, step)
        line = lines[(0, step[1]) if step[1] else step]

        @pl.when(there)
        def _(line=line, place=place):
            lines_ref[owner[place], :thick] = line


def occupied_kernel(owner, raw_ref, mask_ref, out_ref, rows_ref):
    def store(y, rows):
        rows_ref[:, y, :] = rows

    unrolled(raw_ref, mask_ref, store)
    out_ref[...] = rows_ref[...].reshape(out_ref.shape).astype(BF)


def fill_planes(x_ref, planes_ref, lines_ref, rim):
    depth, _, channels = x_ref.shape
    planes_ref[1 : depth + 1] = x_ref[...]
    rim[1 : depth + 1] = x_ref[...].reshape(depth, EDGE, EDGE, channels).astype(F32)
    lines_ref[...] = jnp.zeros(lines_ref.shape, BF)


def lines_kernel(owner, inner_ref, x_ref, outer_ref, lines_ref, planes_ref, rim):
    fill_planes(x_ref, planes_ref, lines_ref, rim)
    cut_lines(owner, inner_ref, outer_ref, lines_ref, planes_ref, rim)


def gather_windows(owner, x_ref, recv_ref, rim, patch):
    thick, _, channels = x_ref.shape
    rim[:, 1:9, 8:16, :] = x_ref[...].reshape(thick, EDGE, EDGE, channels).astype(F32)
    spot = placed_at(owner)
    lines = [
        recv_ref[owner[neighbour(spot, step)[1]], :thick].astype(F32) for step in STEPS
    ]
    rim[:, 1:9, 16, :] = lines[0]
    rim[:, 1:9, 7, :] = lines[1]
    rim[:, 9, 8:16, :] = lines[2]
    rim[:, 0, 8:16, :] = lines[3]
    rim[:, 9, 16, :] = lines[4][:, 0]
    rim[:, 9, 7, :] = lines[5][:, 0]
    rim[:, 0, 16, :] = lines[6][:, 7]
    rim[:, 0, 7, :] = lines[7][:, 7]

    def plane(z, carry):
        for dx in range(3):
            for dy in range(3):
                seen = rim[z, dx : dx + 8, 7 + dy : 15 + dy, :]
                row = pl.multiple_of(z * 64, 64)
                patch[dx * 3 + dy, pl.ds(row, 64), :] = seen.reshape(64, channels).astype(BF)
        return carry

    lax.fori_loop(0, thick, plane, 0)


def forward_kernel(share, regions, n_leaves, owner, x_ref, recv_ref, w_ref, bias_ref,
                   cot_ref, mask_ref, act_ref, gp_ref, gb_ref, gw_ref, rim, patch, cot):
    voxels, channels = gp_ref.shape

    def store(y, rows):
        cot[:, y, :] = rows

    unrolled(cot_ref, mask_ref, store)
    gather_windows(owner, x_ref, recv_ref, rim, patch)
    pre = jnp.broadcast_to(bias_ref[...], (voxels, channels))
    for dz in range(3):
        for k in range(9):
            pre += jnp.dot(
                patch[k, dz * 64 : dz * 64 + voxels, :],
                w_ref[dz * 9 + k],
                preferred_element_type=F32,
            )
    sigma = jax.nn.sigmoid(pre)
    upstream = cot[...].reshape(voxels, channels)
    grad = (upstream * sigma * (1.0 + pre * (1.0 - sigma))).astype(BF)
    gp_ref[...] = grad
    act_ref[...] = (pre * sigma).astype(BF)
    rest = jnp.sum(grad.astype(F32), axis=0, keepdims=True)
    rows = []
    for term in split_in_three(rest):
        tail = jnp.zeros((1, 256 - channels), F32)
        rows += [term[:, :128], jnp.concatenate([term[:, 128:], tail], axis=1)]
    rows.append(jnp.zeros((ROWS - len(rows), 128), F32))
    gb_ref[0] = jnp.concatenate(rows, axis=0).astype(BF)
    half = channels // 2
    per_offset = half // ROWS
    lanes = 2 * channels // 128
    code = leaf_codes(owner.shape[0])

    slab = lax.axis_index("region")

    def put(unit, value):
        part, inner = divmod(unit, share)
        leaf, level = divmod(part, regions)
        colour = (leaf // (n_leaves // 4)) % 2
        gw_ref[((leaf ^ code[colour]) * regions + (level ^ slab)) * share + inner] = value

    for dz in range(3):
        for k in range(9):
            o = dz * 9 + k
            part = lax.dot_general(
                patch[k, dz * 64 : dz * 64 + voxels, :],
                grad,
                (((0,), (0,)), ((), ())),
                preferred_element_type=F32,
            )
            wide = jnp.concatenate([part[:half], part[half:]], axis=1).astype(BF)
            for rows in range(per_offset):
                for lane in range(lanes):
                    put(
                        (o * per_offset + rows) * lanes + lane,
                        wide[rows * ROWS : (rows + 1) * ROWS, lane * 128 : (lane + 1) * 128],
                    )
    for unit in range(27 * per_offset * lanes, share * regions * n_leaves):
        put(unit, jnp.zeros((ROWS, 128), BF))


def input_kernel(owner, x_ref, recv_ref, w_ref, mask_ref, pre_ref, out_ref, act_ref,
                 rim, patch, rows):
    channels = w_ref.shape[1]
    voxels = (x_ref.shape[0] - 2) * 64
    gather_windows(owner, x_ref, recv_ref, rim, patch)
    total = jnp.zeros((voxels, channels), F32)
    for dz in range(3):
        for k in range(9):
            total += lax.dot_general(
                patch[8 - k, (2 - dz) * 64 : (2 - dz) * 64 + voxels, :],
                w_ref[dz * 9 + k],
                (((1,), (1,)), ((), ())),
                preferred_element_type=F32,
            )
    rows[...] = pre_ref[...].astype(F32).reshape(rows.shape)
    act_ref[...] = rolled(rows, mask_ref)
    rows[...] = total.reshape(rows.shape)
    out_ref[...] = rolled(rows, mask_ref)


def unfold_kernel(share, regions, n_leaves, owner, *refs):
    *pieces, out_ref, gb_ref, flat = refs
    code = leaf_codes(owner.shape[0])
    slab = lax.axis_index("region")
    part = 0
    for piece in pieces:
        for first in range(0, regions * share, share):
            rel, level = divmod(part, regions)
            colour = (rel // (n_leaves // 4)) % 2
            row = ((rel ^ code[colour]) * regions + (level ^ slab)) * (share * PITCH)
            for n in range(share):
                flat[pl.ds(row + n * PITCH, ROWS), :] = piece[first + n].astype(F32)
            part += 1
    terms = jnp.zeros((ROWS, 128), F32)
    for piece in pieces:
        if piece.shape[0] > regions * share:
            terms = terms + piece[regions * share].astype(F32)
    low_lanes = terms[0:1] + terms[2:3] + terms[4:5]
    high_lanes = terms[1:2] + terms[3:4] + terms[5:6]
    channels = gb_ref.shape[1]
    gb_ref[...] = jnp.concatenate([low_lanes, high_lanes[:, : channels - 128]], axis=1)
    pitch = out_ref.shape[1] // (128 * ROWS) * PITCH
    low = lax.broadcasted_iota(jnp.int32, (8, 128), 1) < 64

    def turned(x):
        return pltpu.roll(x, 64, 1)

    def block(base, group):
        rows = []
        for i in range(2):
            rows.append(
                [
                    flat[pl.ds(base + i + lane * PITCH + group * 8 * pitch, 8, stride=pitch), :]
                    for lane in range(3)
                ]
            )
        (a0, a1, a2), (b0, b1, b2) = rows
        rb0, rb1, ra1, ra2 = turned(b0), turned(b1), turned(a1), turned(a2)
        return (
            a0,
            jnp.where(low, a1, rb0),
            jnp.where(low, rb0, rb1),
            jnp.where(low, ra1, ra2),
            jnp.where(low, ra2, b1),
            b2,
        )

    count = out_ref.shape[0]
    span = out_ref.shape[1] // 2

    def pair(m, carry):
        i = m * 2
        base = (i // ROWS) * (3 * PITCH) + i % ROWS
        for top in range(0, count, 16):
            tiles = [block(base, top // 8), block(base, top // 8 + 1)]
            high = min(16, count - top)
            for n in range(6):
                both = jnp.concatenate([tiles[0][n], tiles[1][n]], axis=0).astype(BF)
                lane = pl.multiple_of((n // 3) * span + m * 384 + (n % 3) * 128, 128)
                out_ref[top : top + high, pl.ds(lane, 128)] = both[:high]
        return carry

    lax.fori_loop(0, span // 384, pair, 0, unroll=8)


def body(features, mask, owner, weight, bias, cotangent):
    channels = bias.shape[0]
    depth = features.shape[0]
    voxels = depth * 64
    regions = lax.axis_size("region")
    tiles = lax.axis_size("batch")
    bits = tiles.bit_length() - 1
    slab = lax.axis_index("region")
    orders = send_orders(tiles)
    n_leaves = 2 * tiles
    units = 27 * (channels // 2 // ROWS) * (2 * channels // 128)
    leaf_units = -(-units // (n_leaves * regions)) * regions
    share = leaf_units // regions
    barrier = lax.optimization_barrier

    odd = slab & 1
    joined = [[(i, i ^ 1) for i in range(regions)]]
    joined.append([(i, i + 1 - 2 * (1 - i % 2)) for i in range(1, regions - 1)])

    def rims(plane):
        top = depth - 1
        inner = lax.ppermute(plane(top * (1 - odd)), "region", joined[0])
        outer = lax.ppermute(plane(top * odd), "region", joined[1])
        return inner, outer

    def cut(*operands):
        return pl.pallas_call(
            lines_kernel,
            out_shape=(
                jax.ShapeDtypeStruct((tiles, depth + 2, EDGE, channels), BF),
                jax.ShapeDtypeStruct((depth + 2, 64, channels), BF),
            ),
            in_specs=[SMEM] + [VMEM] * len(operands),
            out_specs=(VMEM, VMEM),
            scratch_shapes=[pltpu.VMEM((depth + 2, EDGE, EDGE, channels), F32)],
            compiler_params=vmem(12),
        )(owner, *operands)

    def exchanged(lines):
        return lax.all_to_all(lines, "batch", 0, 0, tiled=True)

    scratch = [
        pltpu.VMEM((depth + 2, 10, 24, channels), F32),
        pltpu.VMEM((9, (depth + 2) * 64, channels), BF),
        pltpu.VMEM((depth * EDGE, EDGE, channels), F32),
    ]
    marks = mask.reshape(depth * EDGE, EDGE)
    flat = (depth * EDGE, EDGE * channels)

    def own_plane(z):
        seen = lax.dynamic_slice_in_dim(features, z, 1, 0).reshape(1, 64, channels)
        kept = lax.dynamic_slice_in_dim(mask, z, 1, 0).reshape(1, 64, 1)
        return seen * kept.astype(BF)

    inner, outer = rims(own_plane)
    occupied = pl.pallas_call(
        occupied_kernel,
        out_shape=jax.ShapeDtypeStruct((depth, 64, channels), BF),
        in_specs=[SMEM, VMEM, VMEM],
        out_specs=VMEM,
        scratch_shapes=[pltpu.VMEM((depth * EDGE, EDGE, channels), F32)],
        compiler_params=vmem(12),
    )(owner, features.reshape(flat), marks)
    lines, planes = cut(inner, occupied, outer)
    lines, weight = barrier((lines, weight))
    arrived = exchanged(lines)
    kernel = weight.reshape(27, channels, channels)

    act, grad, bias_terms, terms = pl.pallas_call(
        functools.partial(forward_kernel, share, regions, n_leaves),
        out_shape=(
            jax.ShapeDtypeStruct((voxels, channels), BF),
            jax.ShapeDtypeStruct((voxels, channels), BF),
            jax.ShapeDtypeStruct((1, ROWS, 128), BF),
            jax.ShapeDtypeStruct((n_leaves * leaf_units, ROWS, 128), BF),
        ),
        in_specs=[SMEM] + [VMEM] * 6,
        out_specs=(VMEM, VMEM, VMEM, VMEM),
        scratch_shapes=scratch,
        compiler_params=vmem(24),
        cost_estimate=pl.CostEstimate(
            flops=4 * 27 * voxels * channels * channels,
            bytes_accessed=6 << 20,
            transcendentals=voxels * channels,
        ),
    )(owner, planes, arrived, kernel, bias.reshape(1, channels), cotangent.reshape(flat), marks)
    grad = grad.reshape(depth, 64, channels)

    def halve(x, axis, count, flip):
        half = x.shape[0] // 2
        got = lax.ppermute(x[half:].astype(BF), axis, pairs(count, flip))
        return x[:half].astype(F32) + got.astype(F32)

    parts = halve(terms, "batch", tiles, 1)
    split = parts.shape[0] // 2
    colours = [parts[:split], parts[split:]]
    inner, outer = rims(lambda z: lax.dynamic_slice_in_dim(grad, z, 1, 0))
    for step in range(bits - 1):
        colours = [halve(c, "batch", tiles, 1 << o[step]) for c, o in zip(colours, orders)]
        if step == 0:
            lines, grad_planes = cut(inner, grad, outer)
            colours, lines = barrier((colours, lines))
            arrived = exchanged(lines)

    def level(k):
        return [c[k * share : (k + 1) * share] for c in colours]

    total = jnp.concatenate(level(0), axis=0)
    gots = []
    for flip in sorted(range(1, regions), key=lambda f: -f):
        sent = jnp.concatenate([x.astype(BF) for x in level(flip)] + [bias_terms], axis=0)
        gots.append(lax.ppermute(sent, "region", pairs(regions, flip)))
        total = total + gots[-1][:-1].astype(F32)
    total = total.astype(BF)
    terms = bias_terms[0].astype(F32) + sum(got[-1].astype(F32) for got in gots)
    terms = jnp.sum(terms[:6].reshape(3, 2, 128), axis=0)
    columns = []
    for _ in range(3):
        columns.append(lax.reduce_precision(terms, 8, 7))
        terms = terms - columns[-1]
    column = jnp.pad(jnp.concatenate(columns, axis=0), ((0, ROWS - 6), (0, 0))).astype(BF)

    held = [total] + [
        lax.ppermute(total, "region", pairs(regions, flip)) for flip in range(1, regions)
    ]
    grad_input, activation = pl.pallas_call(
        input_kernel,
        out_shape=(
            jax.ShapeDtypeStruct(flat, BF),
            jax.ShapeDtypeStruct(flat, BF),
        ),
        in_specs=[SMEM] + [VMEM] * 5,
        out_specs=(VMEM, VMEM),
        scratch_shapes=scratch,
        compiler_params=vmem(20),
        cost_estimate=pl.CostEstimate(
            flops=2 * 27 * voxels * channels * channels, bytes_accessed=3 << 20, transcendentals=0
        ),
    )(owner, grad_planes, arrived, kernel, marks, act)

    held, grad_input, activation = barrier((held, grad_input, activation))
    colours = [
        [jnp.concatenate([h[c * share : (c + 1) * share] for h in held] + [column[None]][c:])]
        for c in range(2)
    ]
    for step in reversed(range(bits - 1)):
        colours = [
            c + [lax.ppermute(x, "batch", pairs(tiles, 1 << o[step])) for x in c]
            for c, o in zip(colours, orders)
        ]
    near = colours[0] + colours[1]
    far = [lax.ppermute(c, "batch", pairs(tiles, 1)) for c in near]
    kernel_grad, total_bias = pl.pallas_call(
        functools.partial(unfold_kernel, share, regions, n_leaves),
        out_shape=(
            jax.ShapeDtypeStruct((27, channels * channels), BF),
            jax.ShapeDtypeStruct((1, channels), F32),
        ),
        in_specs=[SMEM] + [VMEM] * len(near + far),
        out_specs=(VMEM, VMEM),
        scratch_shapes=[pltpu.VMEM((max(32 * units // 27, n_leaves * leaf_units) * PITCH, 128), F32)],
        compiler_params=vmem(20),
    )(owner, *near, *far)

    shape = features.shape
    outs = activation.reshape(shape), grad_input.reshape(shape)
    return *outs, kernel_grad, total_bias.reshape(channels)


def solution(mesh):
    split = P("region", "batch", None)
    return jax.shard_map(
        body,
        mesh=mesh,
        in_specs=(split, P("region", "batch"), P(), P(), P(), split),
        out_specs=(split, split, P(), P()),
        check_vma=False,
    )
```

```python
import functools

import jax
import jax.numpy as jnp
from jax import lax
from jax.experimental import pallas as pl
from jax.experimental.pallas import tpu as pltpu
from jax.sharding import PartitionSpec as P

BF = jnp.bfloat16
F32 = jnp.float32
STEPS = ((0, 1), (0, -1), (1, 0), (-1, 0), (1, 1), (1, -1), (-1, 1), (-1, -1))
EDGE = 8
ROWS = 16
PITCH = 17
VMEM = pl.BlockSpec(memory_space=pltpu.VMEM)
SMEM = pl.BlockSpec(memory_space=pltpu.SMEM)


def vmem(mib):
    return pltpu.CompilerParams(vmem_limit_bytes=mib * 2**20)


def pairs(count, flip):
    return [(i, i ^ flip) for i in range(count)]


def placed_at(owner):
    tiles = owner.shape[0]
    mine = lax.axis_index("batch")
    place = 0
    for q in range(tiles):
        place = place + jnp.where(owner[q] == mine, q, 0)
    return place, tiles // 4, 4


def neighbour(spot, step):
    place, columns, rows = spot
    column = place % columns + step[0]
    row = place // columns + step[1]
    there = (column >= 0) & (column < columns) & (row >= 0) & (row < rows)
    return there, jnp.where(there, place + step[1] * columns + step[0], place)


def leaf_codes(tiles):
    bits = tiles.bit_length() - 1
    mine = lax.axis_index("batch")
    codes = []
    for order in send_orders(tiles):
        code = (mine & 1) << bits
        for n, bit in enumerate(order):
            code = code | (((mine >> bit) & 1) << (bits - 2 - n))
        codes.append(code)
    return codes


def send_orders(tiles):
    bits = tiles.bit_length() - 1
    return tuple(range(1, bits)), tuple(range(bits - 1, 0, -1))


def split_in_three(x):
    terms = []
    for _ in range(3):
        terms.append(x.astype(BF).astype(F32))
        x = x - terms[-1]
    return terms


def unrolled(raw_ref, mask_ref, store):
    count = mask_ref.shape[1]
    wide = raw_ref[...].astype(F32)
    kept = mask_ref[...].astype(F32)
    channels = wide.shape[1] // count
    for y in range(count):
        store(y, wide[:, y * channels : (y + 1) * channels] * kept[:, y : y + 1])


def rolled(rows, mask_ref):
    kept = mask_ref[...].astype(F32)
    parts = [rows[:, y, :] * kept[:, y : y + 1] for y in range(mask_ref.shape[1])]
    return jnp.concatenate(parts, axis=1).astype(BF)


def cut_lines(owner, inner_ref, outer_ref, lines_ref, planes_ref, rim):
    thick, _, _, channels = rim.shape
    odd = lax.axis_index("region") & 1
    for ref, z in ((inner_ref, (thick - 1) * (1 - odd)), (outer_ref, (thick - 1) * odd)):
        planes_ref[z] = ref[0]
        rim[z] = ref[0].reshape(EDGE, EDGE, channels).astype(F32)
    spot = placed_at(owner)
    lines = {
        (0, 1): rim[:, :, 7, :].astype(BF),
        (0, -1): rim[:, :, 0, :].astype(BF),
        (1, 0): rim[:, 7].astype(BF),
        (-1, 0): rim[:, 0].astype(BF),
    }
    for step in STEPS:
        there, place = neighbour(spot, step)
        line = lines[(0, step[1]) if step[1] else step]

        @pl.when(there)
        def _(line=line, place=place):
            lines_ref[owner[place], :thick] = line


def occupied_kernel(owner, raw_ref, mask_ref, out_ref, rows_ref):
    def store(y, rows):
        rows_ref[:, y, :] = rows

    unrolled(raw_ref, mask_ref, store)
    out_ref[...] = rows_ref[...].reshape(out_ref.shape).astype(BF)


def fill_planes(x_ref, planes_ref, lines_ref, rim):
    depth, _, channels = x_ref.shape
    planes_ref[1 : depth + 1] = x_ref[...]
    rim[1 : depth + 1] = x_ref[...].reshape(depth, EDGE, EDGE, channels).astype(F32)
    lines_ref[...] = jnp.zeros(lines_ref.shape, BF)


def lines_kernel(owner, inner_ref, x_ref, outer_ref, lines_ref, planes_ref, rim):
    fill_planes(x_ref, planes_ref, lines_ref, rim)
    cut_lines(owner, inner_ref, outer_ref, lines_ref, planes_ref, rim)


def gather_windows(owner, x_ref, recv_ref, rim, patch):
    thick, _, channels = x_ref.shape
    rim[:, 1:9, 8:16, :] = x_ref[...].reshape(thick, EDGE, EDGE, channels).astype(F32)
    spot = placed_at(owner)
    lines = [
        recv_ref[owner[neighbour(spot, step)[1]], :thick].astype(F32) for step in STEPS
    ]
    rim[:, 1:9, 16, :] = lines[0]
    rim[:, 1:9, 7, :] = lines[1]
    rim[:, 9, 8:16, :] = lines[2]
    rim[:, 0, 8:16, :] = lines[3]
    rim[:, 9, 16, :] = lines[4][:, 0]
    rim[:, 9, 7, :] = lines[5][:, 0]
    rim[:, 0, 16, :] = lines[6][:, 7]
    rim[:, 0, 7, :] = lines[7][:, 7]

    def plane(z, carry):
        for dx in range(3):
            for dy in range(3):
                seen = rim[z, dx : dx + 8, 7 + dy : 15 + dy, :]
                row = pl.multiple_of(z * 64, 64)
                patch[dx * 3 + dy, pl.ds(row, 64), :] = seen.reshape(64, channels).astype(BF)
        return carry

    lax.fori_loop(0, thick, plane, 0)


def forward_kernel(share, regions, n_leaves, owner, x_ref, recv_ref, w_ref, bias_ref,
                   cot_ref, mask_ref, act_ref, gp_ref, gb_ref, gw_ref, rim, patch, cot):
    voxels, channels = gp_ref.shape

    def store(y, rows):
        cot[:, y, :] = rows

    unrolled(cot_ref, mask_ref, store)
    gather_windows(owner, x_ref, recv_ref, rim, patch)
    pre = jnp.broadcast_to(bias_ref[...], (voxels, channels))
    for dz in range(3):
        for k in range(9):
            pre += jnp.dot(
                patch[k, dz * 64 : dz * 64 + voxels, :],
                w_ref[dz * 9 + k],
                preferred_element_type=F32,
            )
    sigma = jax.nn.sigmoid(pre)
    upstream = cot[...].reshape(voxels, channels)
    grad = (upstream * sigma * (1.0 + pre * (1.0 - sigma))).astype(BF)
    gp_ref[...] = grad
    act_ref[...] = (pre * sigma).astype(BF)
    rest = jnp.sum(grad.astype(F32), axis=0, keepdims=True)
    rows = []
    for term in split_in_three(rest):
        tail = jnp.zeros((1, 256 - channels), F32)
        rows += [term[:, :128], jnp.concatenate([term[:, 128:], tail], axis=1)]
    rows.append(jnp.zeros((ROWS - len(rows), 128), F32))
    gb_ref[0] = jnp.concatenate(rows, axis=0).astype(BF)
    half = channels // 2
    per_offset = half // ROWS
    lanes = 2 * channels // 128
    code = leaf_codes(owner.shape[0])

    slab = lax.axis_index("region")

    def put(unit, value):
        part, inner = divmod(unit, share)
        leaf, level = divmod(part, regions)
        colour = (leaf // (n_leaves // 4)) % 2
        gw_ref[((leaf ^ code[colour]) * regions + (level ^ slab)) * share + inner] = value

    for dz in range(3):
        for k in range(9):
            o = dz * 9 + k
            part = lax.dot_general(
                patch[k, dz * 64 : dz * 64 + voxels, :],
                grad,
                (((0,), (0,)), ((), ())),
                preferred_element_type=F32,
            )
            wide = jnp.concatenate([part[:half], part[half:]], axis=1).astype(BF)
            for rows in range(per_offset):
                for lane in range(lanes):
                    put(
                        (o * per_offset + rows) * lanes + lane,
                        wide[rows * ROWS : (rows + 1) * ROWS, lane * 128 : (lane + 1) * 128],
                    )
    for unit in range(27 * per_offset * lanes, share * regions * n_leaves):
        put(unit, jnp.zeros((ROWS, 128), BF))


def input_kernel(owner, x_ref, recv_ref, w_ref, mask_ref, pre_ref, out_ref, act_ref,
                 rim, patch, rows):
    channels = w_ref.shape[1]
    voxels = (x_ref.shape[0] - 2) * 64
    gather_windows(owner, x_ref, recv_ref, rim, patch)
    total = jnp.zeros((voxels, channels), F32)
    for dz in range(3):
        for k in range(9):
            total += lax.dot_general(
                patch[8 - k, (2 - dz) * 64 : (2 - dz) * 64 + voxels, :],
                w_ref[dz * 9 + k],
                (((1,), (1,)), ((), ())),
                preferred_element_type=F32,
            )
    rows[...] = pre_ref[...].astype(F32).reshape(rows.shape)
    act_ref[...] = rolled(rows, mask_ref)
    rows[...] = total.reshape(rows.shape)
    out_ref[...] = rolled(rows, mask_ref)


def unfold_kernel(share, regions, n_leaves, owner, *refs):
    *pieces, out_ref, gb_ref, flat = refs
    code = leaf_codes(owner.shape[0])
    slab = lax.axis_index("region")
    part = 0
    for piece in pieces:
        for first in range(0, regions * share, share):
            rel, level = divmod(part, regions)
            colour = (rel // (n_leaves // 4)) % 2
            row = ((rel ^ code[colour]) * regions + (level ^ slab)) * (share * PITCH)
            for n in range(share):
                flat[pl.ds(row + n * PITCH, ROWS), :] = piece[first + n].astype(F32)
            part += 1
    terms = jnp.zeros((ROWS, 128), F32)
    for piece in pieces:
        if piece.shape[0] > regions * share:
            terms = terms + piece[regions * share].astype(F32)
    low_lanes = terms[0:1] + terms[2:3] + terms[4:5]
    high_lanes = terms[1:2] + terms[3:4] + terms[5:6]
    channels = gb_ref.shape[1]
    gb_ref[...] = jnp.concatenate([low_lanes, high_lanes[:, : channels - 128]], axis=1)
    pitch = out_ref.shape[1] // (128 * ROWS) * PITCH
    low = lax.broadcasted_iota(jnp.int32, (8, 128), 1) < 64

    def turned(x):
        return pltpu.roll(x, 64, 1)

    def block(base, group):
        rows = []
        for i in range(2):
            rows.append(
                [
                    flat[pl.ds(base + i + lane * PITCH + group * 8 * pitch, 8, stride=pitch), :]
                    for lane in range(3)
                ]
            )
        (a0, a1, a2), (b0, b1, b2) = rows
        rb0, rb1, ra1, ra2 = turned(b0), turned(b1), turned(a1), turned(a2)
        return (
            a0,
            jnp.where(low, a1, rb0),
            jnp.where(low, rb0, rb1),
            jnp.where(low, ra1, ra2),
            jnp.where(low, ra2, b1),
            b2,
        )

    count = out_ref.shape[0]
    span = out_ref.shape[1] // 2

    def pair(m, carry):
        i = m * 2
        base = (i // ROWS) * (3 * PITCH) + i % ROWS
        for top in range(0, count, 16):
            tiles = [block(base, top // 8), block(base, top // 8 + 1)]
            high = min(16, count - top)
            for n in range(6):
                both = jnp.concatenate([tiles[0][n], tiles[1][n]], axis=0).astype(BF)
                lane = pl.multiple_of((n // 3) * span + m * 384 + (n % 3) * 128, 128)
                out_ref[top : top + high, pl.ds(lane, 128)] = both[:high]
        return carry

    lax.fori_loop(0, span // 384, pair, 0, unroll=16)


def body(features, mask, owner, weight, bias, cotangent):
    channels = bias.shape[0]
    depth = features.shape[0]
    voxels = depth * 64
    regions = lax.axis_size("region")
    tiles = lax.axis_size("batch")
    bits = tiles.bit_length() - 1
    slab = lax.axis_index("region")
    orders = send_orders(tiles)
    n_leaves = 2 * tiles
    units = 27 * (channels // 2 // ROWS) * (2 * channels // 128)
    leaf_units = -(-units // (n_leaves * regions)) * regions
    share = leaf_units // regions
    barrier = lax.optimization_barrier

    odd = slab & 1
    joined = [[(i, i ^ 1) for i in range(regions)]]
    joined.append([(i, i + 1 - 2 * (1 - i % 2)) for i in range(1, regions - 1)])

    def rims(plane):
        top = depth - 1
        inner = lax.ppermute(plane(top * (1 - odd)), "region", joined[0])
        outer = lax.ppermute(plane(top * odd), "region", joined[1])
        return inner, outer

    def cut(*operands):
        return pl.pallas_call(
            lines_kernel,
            out_shape=(
                jax.ShapeDtypeStruct((tiles, depth + 2, EDGE, channels), BF),
                jax.ShapeDtypeStruct((depth + 2, 64, channels), BF),
            ),
            in_specs=[SMEM] + [VMEM] * len(operands),
            out_specs=(VMEM, VMEM),
            scratch_shapes=[pltpu.VMEM((depth + 2, EDGE, EDGE, channels), F32)],
            compiler_params=vmem(12),
        )(owner, *operands)

    def exchanged(lines):
        return lax.all_to_all(lines, "batch", 0, 0, tiled=True)

    scratch = [
        pltpu.VMEM((depth + 2, 10, 24, channels), F32),
        pltpu.VMEM((9, (depth + 2) * 64, channels), BF),
        pltpu.VMEM((depth * EDGE, EDGE, channels), F32),
    ]
    marks = mask.reshape(depth * EDGE, EDGE)
    flat = (depth * EDGE, EDGE * channels)

    def own_plane(z):
        seen = lax.dynamic_slice_in_dim(features, z, 1, 0).reshape(1, 64, channels)
        kept = lax.dynamic_slice_in_dim(mask, z, 1, 0).reshape(1, 64, 1)
        return seen * kept.astype(BF)

    inner, outer = rims(own_plane)
    occupied = pl.pallas_call(
        occupied_kernel,
        out_shape=jax.ShapeDtypeStruct((depth, 64, channels), BF),
        in_specs=[SMEM, VMEM, VMEM],
        out_specs=VMEM,
        scratch_shapes=[pltpu.VMEM((depth * EDGE, EDGE, channels), F32)],
        compiler_params=vmem(12),
    )(owner, features.reshape(flat), marks)
    lines, planes = cut(inner, occupied, outer)
    lines, weight = barrier((lines, weight))
    arrived = exchanged(lines)
    kernel = weight.reshape(27, channels, channels)

    act, grad, bias_terms, terms = pl.pallas_call(
        functools.partial(forward_kernel, share, regions, n_leaves),
        out_shape=(
            jax.ShapeDtypeStruct((voxels, channels), BF),
            jax.ShapeDtypeStruct((voxels, channels), BF),
            jax.ShapeDtypeStruct((1, ROWS, 128), BF),
            jax.ShapeDtypeStruct((n_leaves * leaf_units, ROWS, 128), BF),
        ),
        in_specs=[SMEM] + [VMEM] * 6,
        out_specs=(VMEM, VMEM, VMEM, VMEM),
        scratch_shapes=scratch,
        compiler_params=vmem(24),
        cost_estimate=pl.CostEstimate(
            flops=4 * 27 * voxels * channels * channels,
            bytes_accessed=6 << 20,
            transcendentals=voxels * channels,
        ),
    )(owner, planes, arrived, kernel, bias.reshape(1, channels), cotangent.reshape(flat), marks)
    grad = grad.reshape(depth, 64, channels)

    def halve(x, axis, count, flip):
        half = x.shape[0] // 2
        got = lax.ppermute(x[half:].astype(BF), axis, pairs(count, flip))
        return x[:half].astype(F32) + got.astype(F32)

    parts = halve(terms, "batch", tiles, 1)
    split = parts.shape[0] // 2
    colours = [parts[:split], parts[split:]]
    inner, outer = rims(lambda z: lax.dynamic_slice_in_dim(grad, z, 1, 0))
    for step in range(bits - 1):
        colours = [halve(c, "batch", tiles, 1 << o[step]) for c, o in zip(colours, orders)]
        if step == 0:
            lines, grad_planes = cut(inner, grad, outer)
            colours, lines = barrier((colours, lines))
            arrived = exchanged(lines)

    def level(k):
        return [c[k * share : (k + 1) * share] for c in colours]

    total = jnp.concatenate(level(0), axis=0)
    gots = []
    for flip in sorted(range(1, regions), key=lambda f: -f):
        sent = jnp.concatenate([x.astype(BF) for x in level(flip)] + [bias_terms], axis=0)
        gots.append(lax.ppermute(sent, "region", pairs(regions, flip)))
        total = total + gots[-1][:-1].astype(F32)
    total = total.astype(BF)
    terms = bias_terms[0].astype(F32) + sum(got[-1].astype(F32) for got in gots)
    terms = jnp.sum(terms[:6].reshape(3, 2, 128), axis=0)
    columns = []
    for _ in range(3):
        columns.append(lax.reduce_precision(terms, 8, 7))
        terms = terms - columns[-1]
    column = jnp.pad(jnp.concatenate(columns, axis=0), ((0, ROWS - 6), (0, 0))).astype(BF)

    held = [total] + [
        lax.ppermute(total, "region", pairs(regions, flip)) for flip in range(1, regions)
    ]
    grad_input, activation = pl.pallas_call(
        input_kernel,
        out_shape=(
            jax.ShapeDtypeStruct(flat, BF),
            jax.ShapeDtypeStruct(flat, BF),
        ),
        in_specs=[SMEM] + [VMEM] * 5,
        out_specs=(VMEM, VMEM),
        scratch_shapes=scratch,
        compiler_params=vmem(20),
        cost_estimate=pl.CostEstimate(
            flops=2 * 27 * voxels * channels * channels, bytes_accessed=3 << 20, transcendentals=0
        ),
    )(owner, grad_planes, arrived, kernel, marks, act)

    held, grad_input, activation = barrier((held, grad_input, activation))
    colours = [
        [jnp.concatenate([h[c * share : (c + 1) * share] for h in held] + [column[None]][c:])]
        for c in range(2)
    ]
    for step in reversed(range(bits - 1)):
        colours = [
            c + [lax.ppermute(x, "batch", pairs(tiles, 1 << o[step])) for x in c]
            for c, o in zip(colours, orders)
        ]
    near = colours[0] + colours[1]
    far = [lax.ppermute(c, "batch", pairs(tiles, 1)) for c in near]
    kernel_grad, total_bias = pl.pallas_call(
        functools.partial(unfold_kernel, share, regions, n_leaves),
        out_shape=(
            jax.ShapeDtypeStruct((27, channels * channels), BF),
            jax.ShapeDtypeStruct((1, channels), F32),
        ),
        in_specs=[SMEM] + [VMEM] * len(near + far),
        out_specs=(VMEM, VMEM),
        scratch_shapes=[pltpu.VMEM((max(32 * units // 27, n_leaves * leaf_units) * PITCH, 128), F32)],
        compiler_params=vmem(20),
    )(owner, *near, *far)

    shape = features.shape
    outs = activation.reshape(shape), grad_input.reshape(shape)
    return *outs, kernel_grad, total_bias.reshape(channels)


def solution(mesh):
    split = P("region", "batch", None)
    return jax.shard_map(
        body,
        mesh=mesh,
        in_specs=(split, P("region", "batch"), P(), P(), P(), split),
        out_specs=(split, split, P(), P()),
        check_vma=False,
    )
```
